512 devices in a mesh: img: 16 (over z, core), txt: 32 (over x, y).
Axes of the slice: x: 4, y: 8, z: 8, core: 2. Of those that a mesh axis runs over, the one named last changes fastest.
Arguments:
- images: bfloat16 [16384, 1024], P('img', 'txt'), may hold values from -4 to 4
- texts: bfloat16 [16384, 1024], P('txt', 'img'), may hold values from -4 to 4
- positive: int32 [16384], P('img'), may hold values from 0 to 16383, each once
- scale_logarithm: float32 [1], replicated, may hold values from 2.3 to 3
Outputs:
- loss: float32 [1], replicated
- grad_images: bfloat16 [16384, 1024], P('img', 'txt')
- grad_texts: bfloat16 [16384, 1024], P('txt', 'img')
- grad_log_scale: float32 [1], replicated
The draws below stay inside these ranges and needn't reach their ends.
Inputs may be any that keep to these rules, and one draw needn't show every extreme that they name: `positive`: a permutation of 0 to 16383.
All inputs are finite; a program needn't handle non-finite values.
Results may differ from the reference program's by a relative error of at most 0.019.
Values may be sent and summed in bfloat16 or wider, within the bound.
No kernel may reach another device: no remote copies, remote signals or barrier semaphores. Data moves between devices by JAX's collectives and lax.ppermute only.
A program may use at most 64 MiB of HBM per device.

```python
import math
import jax
import jax.numpy as jnp
from jax import lax

D = 1024
BATCH = 16384
N_IMG = 16
N_TXT = 32


def embedding_draw(noise_key, scale_key):
    row_ids = jnp.arange(BATCH)[:, None]
    spread = jnp.exp(jax.random.uniform(scale_key, (BATCH, 1), jnp.float32, 0.0, math.log(3.2)))
    scales = spread * (1.0 + row_ids.astype(jnp.float32) / BATCH)
    noise = jax.random.truncated_normal(noise_key, -4.0, 4.0, (BATCH, D), jnp.float32)
    return noise * scales / math.sqrt(D)


def draw_images(key, part):
    key = jax.random.fold_in(key, 11)
    noise_key, scale_key = jax.random.split(key)
    values = embedding_draw(noise_key, scale_key)
    return values.astype(jnp.bfloat16)


def draw_texts(key, part):
    key = jax.random.fold_in(key, 12)
    noise_key, scale_key = jax.random.split(key)
    values = embedding_draw(noise_key, scale_key)
    return values.astype(jnp.bfloat16)


def setup_inputs(seed: int = 0) -> dict:
    key_of = jax.random.split(jax.random.key(seed), 5)
    return {
        "images": draw_images(jax.random.fold_in(key_of[4], 71), 0),
        "texts": draw_texts(jax.random.fold_in(key_of[4], 71), 0),
        "positive": jax.random.permutation(key_of[2], BATCH).astype(jnp.int32),
        "scale_logarithm": jnp.clip(jax.random.uniform(key_of[3], (1,), jnp.float32, 2.3, 3.0), 2.3, 3.0),
    }


def reference(images, texts, positive, scale_logarithm):
    logit_multiplier = jnp.exp(scale_logarithm[0].astype(jnp.float32))
    row_tile_block = BATCH // N_IMG
    column_tile_block = BATCH // N_TXT

    def row_logsum(image_tile_block):
        logit_matrix = logit_multiplier * jnp.dot(image_tile_block, texts.T, preferred_element_type=jnp.float32)
        highest = jnp.max(logit_matrix, axis=1, keepdims=True)
        return highest[:, 0] + jnp.log(jnp.sum(jnp.exp(logit_matrix - highest), axis=1))

    def column_logsum(text_tile_block):
        logit_matrix = logit_multiplier * jnp.dot(text_tile_block, images.T, preferred_element_type=jnp.float32)
        highest = jnp.max(logit_matrix, axis=1, keepdims=True)
        return highest[:, 0] + jnp.log(jnp.sum(jnp.exp(logit_matrix - highest), axis=1))

    row_norms = lax.map(row_logsum, images.reshape(N_IMG, row_tile_block, D)).reshape(BATCH)
    column_norms = lax.map(column_logsum, texts.reshape(N_TXT, column_tile_block, D)).reshape(BATCH)
    paired_logit = texts[positive]
    positive_logit_sum = logit_multiplier * jnp.sum(images.astype(jnp.float32) * paired_logit.astype(jnp.float32))
    loss = (0.5 * (jnp.sum(row_norms) + jnp.sum(column_norms)) - positive_logit_sum) / BATCH
    image_loss_pieces = images.reshape(N_IMG, row_tile_block, D).astype(jnp.float32)

    def sweep(carry, column_index):
        accum, slope = carry
        offset = (column_index * column_tile_block).astype(jnp.int32)
        text_tile_block = lax.dynamic_slice_in_dim(texts, offset, column_tile_block, 0)
        norms_here = lax.dynamic_slice_in_dim(column_norms, offset, column_tile_block, 0)
        logit_matrix = logit_multiplier * jnp.dot(images, text_tile_block.T, preferred_element_type=jnp.float32)
        column_ids = offset + jnp.arange(column_tile_block, dtype=jnp.int32)
        matched = (positive[:, None] == column_ids[None, :]).astype(jnp.float32)
        weights = 0.5 * (jnp.exp(logit_matrix - row_norms[:, None]) + jnp.exp(logit_matrix - norms_here[None, :])) - matched
        slope = slope + jnp.sum(weights * logit_matrix)
        weights_reduced_precision = weights.astype(jnp.bfloat16)
        image_loss_entry = logit_multiplier * jnp.dot(weights_reduced_precision, text_tile_block, preferred_element_type=jnp.float32)
        accum = accum + lax.optimization_barrier(image_loss_entry.astype(jnp.bfloat16)).astype(jnp.float32)
        text_loss_entries = logit_multiplier * jnp.einsum("ilz,ilg->izg", weights_reduced_precision.reshape(N_IMG, row_tile_block, column_tile_block).astype(jnp.float32), image_loss_pieces)
        text_grad = jnp.sum(lax.optimization_barrier(text_loss_entries.astype(jnp.bfloat16)).astype(jnp.float32), axis=0)
        return (accum, slope), text_grad.astype(jnp.bfloat16)

    start_carry = (jnp.zeros((BATCH, D), jnp.float32), jnp.zeros((), jnp.float32))
    (accum, slope), text_grads = lax.scan(sweep, start_carry, jnp.arange(N_TXT, dtype=jnp.int32))
    grad_images = accum.astype(jnp.bfloat16)
    grad_texts = text_grads.reshape(BATCH, D)
    return loss.reshape(1), grad_images, grad_texts, (slope / BATCH).reshape(1)
```

```python
import jax
import jax.numpy as jnp
from jax import lax
from jax.sharding import PartitionSpec as P

X_CHIPS = 4
Y_CHIPS = 8
ALONG_Y = [[x * Y_CHIPS + y for y in range(Y_CHIPS)] for x in range(X_CHIPS)]
ALONG_X = [[x * Y_CHIPS + y for x in range(X_CHIPS)] for y in range(Y_CHIPS)]


def exchange(blocks, axis, groups=None):
    return lax.all_to_all(blocks, axis, 0, 0, axis_index_groups=groups)


def collect(block, axis, count, groups=None):
    return exchange(jnp.broadcast_to(block[None], (count,) + block.shape), axis, groups)


def local_softmax(logits, axis):
    high = jnp.max(logits, axis=axis, keepdims=True)
    powers = jnp.exp(logits - high)
    total = jnp.sum(powers, axis=axis)
    mean = jnp.sum(powers * logits, axis=axis) / total
    return jnp.squeeze(high, axis) + jnp.log(total), mean


def merge(norms, means):
    high = jnp.max(norms, axis=0)
    powers = jnp.exp(norms - high)
    total = jnp.sum(powers, axis=0)
    return high + jnp.log(total), jnp.sum(jnp.sum(powers * means, axis=0) / total)


def per_device(images, texts, positive, scale_logarithm):
    n_img, n_txt = lax.axis_size("img"), lax.axis_size("txt")
    rows, cols = images.shape[0], texts.shape[0]
    width = images.shape[1] * n_txt
    scale = jnp.exp(scale_logarithm[0])

    text_full = lax.all_gather(texts, "img", axis=1, tiled=True)
    by_y = collect(images.T, "txt", Y_CHIPS, ALONG_Y)
    image_t = collect(by_y, "txt", X_CHIPS, ALONG_X).reshape(width, rows)

    logits = scale * lax.dot_general(
        image_t, text_full, (((0,), (1,)), ((), ())), preferred_element_type=jnp.float32
    )
    column_ids = lax.axis_index("txt") * cols + jnp.arange(cols, dtype=jnp.int32)
    matched = (positive[:, None] == column_ids[None, :]).astype(jnp.float32)

    col_norm, col_mean = local_softmax(logits, 0)
    row_norm, row_mean = local_softmax(logits, 1)
    matched_sum = jnp.sum(matched * logits)

    packed = jnp.concatenate([col_norm, col_mean, jnp.full((128,), matched_sum)])
    seen = collect(packed[None], "img", n_img)[:, 0]
    column_norms, col_slope = merge(seen[:, :cols], seen[:, cols : 2 * cols])
    matched_here = jnp.sum(seen[:, 2 * cols])
    col_loss = 0.5 * jnp.sum(column_norms) - matched_here
    col_slope = 0.5 * col_slope - matched_here

    packed = jnp.concatenate(
        [row_norm, row_mean, jnp.full((128,), col_loss), jnp.full((128,), col_slope)]
    )
    seen = collect(packed[None], "txt", n_txt)[:, 0]
    row_norms, row_slope = merge(seen[:, :rows], seen[:, rows : 2 * rows])
    col_loss_all = jnp.sum(seen[:, 2 * rows])
    col_slope_all = jnp.sum(seen[:, 2 * rows + 128])

    packed = jnp.concatenate(
        [jnp.full((128,), 0.5 * jnp.sum(row_norms)), jnp.full((128,), 0.5 * row_slope)]
    )
    seen = collect(packed[None], "img", n_img)[:, 0]
    batch = rows * n_img
    loss = ((jnp.sum(seen[:, 0]) + col_loss_all) / batch).reshape(1)
    grad_log_scale = ((jnp.sum(seen[:, 128]) + col_slope_all) / batch).reshape(1)

    weights = (
        0.5 * (jnp.exp(logits - row_norms[:, None]) + jnp.exp(logits - column_norms[None, :]))
        - matched
    ).astype(jnp.bfloat16)

    text_part = scale * lax.dot_general(
        weights, image_t, (((0,), (1,)), ((), ())), preferred_element_type=jnp.float32
    )
    grad_texts = lax.psum_scatter(
        text_part.astype(jnp.bfloat16), "img", scatter_dimension=1, tiled=True
    )

    image_part = scale * lax.dot_general(
        text_full, weights, (((0,), (1,)), ((), ())), preferred_element_type=jnp.float32
    )
    image_part = image_part.astype(jnp.bfloat16).reshape(X_CHIPS, width // X_CHIPS, rows)
    over_x = exchange(image_part, "txt", ALONG_X)
    over_x = jnp.sum(over_x.astype(jnp.float32), axis=0).astype(jnp.bfloat16)
    over_y = exchange(over_x.reshape(Y_CHIPS, -1, rows), "txt", ALONG_Y)
    grad_images = jnp.sum(over_y.astype(jnp.float32), axis=0).astype(jnp.bfloat16).T
    return (loss, grad_images, grad_texts, grad_log_scale)


def solution(mesh):
    return jax.shard_map(
        per_device,
        mesh=mesh,
        in_specs=(P("img", "txt"), P("txt", "img"), P("img"), P()),
        out_specs=(P(), P("img", "txt"), P("txt", "img"), P()),
        check_vma=False,
    )
```

```python
import jax
import jax.numpy as jnp
from jax import lax
from jax.sharding import PartitionSpec as P

X_CHIPS = 4
Y_PAIRS = 4
CORES = 2
PAIRS = [
    [(x * Y_PAIRS + pair) * 2 + side for pair in range(Y_PAIRS)]
    for x in range(X_CHIPS)
    for side in range(2)
]
SQUARES = [
    [(x * Y_PAIRS + pair) * 2 + side for x in range(X_CHIPS) for side in range(2)]
    for pair in range(Y_PAIRS)
]
BOTH_CORES = [[z * CORES + core for core in range(CORES)] for z in range(8)]
ALONG_Z = [[z * CORES + core for z in range(8)] for core in range(CORES)]


def exchange(blocks, axis, groups=None):
    return lax.all_to_all(blocks, axis, 0, 0, axis_index_groups=groups)


def collect(block, axis, count, groups=None):
    return exchange(jnp.broadcast_to(block[None], (count,) + block.shape), axis, groups)


def local_softmax(logits, axis):
    high = jnp.max(logits, axis=axis, keepdims=True)
    powers = jnp.exp(logits - high)
    total = jnp.sum(powers, axis=axis)
    mean = jnp.sum(powers * logits, axis=axis) / total
    return jnp.squeeze(high, axis) + jnp.log(total), mean


def merge(norms):
    high = jnp.max(norms, axis=0)
    return high + jnp.log(jnp.sum(jnp.exp(norms - high), axis=0))


def per_device(images, texts, positive, scale_logarithm):
    n_img, n_txt = lax.axis_size("img"), lax.axis_size("txt")
    rows, cols = images.shape[0], texts.shape[0]
    width = images.shape[1] * n_txt
    scale = jnp.exp(scale_logarithm[0])

    by_core = collect(texts.T, "img", CORES, BOTH_CORES).reshape(-1, cols)
    text_t = lax.all_gather(by_core, "img", axis=0, axis_index_groups=ALONG_Z, tiled=True)
    by_pair = collect(images.T, "txt", Y_PAIRS, PAIRS)
    by_square = collect(by_pair, "txt", 2 * X_CHIPS, SQUARES)
    image_t = by_square.reshape(X_CHIPS, 2, Y_PAIRS, -1, rows).swapaxes(1, 2).reshape(width, rows)

    logits = scale * lax.dot_general(
        image_t, text_t, (((0,), (0,)), ((), ())), preferred_element_type=jnp.float32
    )
    column_ids = lax.axis_index("txt") * cols + jnp.arange(cols, dtype=jnp.int32)
    matched = (positive[:, None] == column_ids[None, :]).astype(jnp.float32)

    col_norm, col_mean = local_softmax(logits, 0)
    row_norm, row_mean = local_softmax(logits, 1)
    matched_sum = jnp.sum(matched * logits)

    seen = collect(row_norm[None], "txt", n_txt)[:, 0]
    row_norms = merge(seen)
    row_slope = jnp.sum(jnp.exp(row_norm - row_norms) * row_mean)

    packed = jnp.concatenate(
        [
            col_norm,
            col_mean,
            jnp.full((128,), 0.5 * jnp.sum(row_norms)),
            jnp.full((128,), 0.5 * row_slope - matched_sum),
            jnp.full((128,), matched_sum),
        ]
    )
    seen = collect(packed[None], "img", n_img)[:, 0]
    column_norms = merge(seen[:, :cols])
    col_slope = jnp.sum(jnp.exp(seen[:, :cols] - column_norms) * seen[:, cols : 2 * cols])
    row_loss_all = jnp.sum(seen[:, 2 * cols])
    slope_here = 0.5 * col_slope + jnp.sum(seen[:, 2 * cols + 128])
    loss_here = 0.5 * jnp.sum(column_norms) - jnp.sum(seen[:, 2 * cols + 256])

    packed = jnp.concatenate([jnp.full((128,), loss_here), jnp.full((128,), slope_here)])
    seen = collect(packed[None], "txt", n_txt)[:, 0]
    batch = rows * n_img
    loss = ((jnp.sum(seen[:, 0]) + row_loss_all) / batch).reshape(1)
    grad_log_scale = (jnp.sum(seen[:, 128]) / batch).reshape(1)

    weights = (
        0.5 * (jnp.exp(logits - row_norms[:, None]) + jnp.exp(logits - column_norms[None, :]))
        - matched
    ).astype(jnp.bfloat16)

    text_part = scale * lax.dot_general(
        image_t, weights, (((1,), (0,)), ((), ())), preferred_element_type=jnp.float32
    )
    text_part = text_part.astype(jnp.bfloat16).reshape(8, CORES, -1, cols).swapaxes(0, 1)
    text_part = jnp.sum(exchange(text_part, "img", BOTH_CORES).astype(jnp.float32), axis=0)
    grad_texts = lax.psum_scatter(
        text_part.astype(jnp.bfloat16).reshape(-1, cols),
        "img",
        scatter_dimension=0,
        axis_index_groups=ALONG_Z,
        tiled=True,
    ).T

    text_t = text_t.reshape(X_CHIPS, Y_PAIRS, 2, -1, cols).swapaxes(1, 2).reshape(width, cols)
    image_part = scale * lax.dot_general(
        text_t, weights, (((1,), (1,)), ((), ())), preferred_element_type=jnp.float32
    )
    image_part = image_part.astype(jnp.bfloat16).reshape(2 * X_CHIPS, -1, rows)
    partial = jnp.sum(exchange(image_part, "txt", SQUARES).astype(jnp.float32), axis=0)
    partial = partial.astype(jnp.bfloat16).reshape(Y_PAIRS, -1, rows)
    partial = jnp.sum(exchange(partial, "txt", PAIRS).astype(jnp.float32), axis=0)
    grad_images = partial.astype(jnp.bfloat16).T
    return (loss, grad_images, grad_texts, grad_log_scale)


def solution(mesh):
    return jax.shard_map(
        per_device,
        mesh=mesh,
        in_specs=(P("img", "txt"), P("txt", "img"), P("img"), P()),
        out_specs=(P(), P("img", "txt"), P("txt", "img"), P()),
        check_vma=False,
    )
```

```python
import jax
import jax.numpy as jnp
from jax import lax
from jax.sharding import PartitionSpec as P

X_CHIPS = 4
Y_PAIRS = 4
CORES = 2
PAIRS = [
    [(x * Y_PAIRS + pair) * 2 + side for pair in range(Y_PAIRS)]
    for x in range(X_CHIPS)
    for side in range(2)
]
SQUARES = [
    [(x * Y_PAIRS + pair) * 2 + side for x in range(X_CHIPS) for side in range(2)]
    for pair in range(Y_PAIRS)
]
BOTH_CORES = [[z * CORES + core for core in range(CORES)] for z in range(8)]
ALONG_Z = [[z * CORES + core for z in range(8)] for core in range(CORES)]


def exchange(blocks, axis, groups=None):
    return lax.all_to_all(blocks, axis, 0, 0, axis_index_groups=groups)


def collect(block, axis, count, groups=None):
    return exchange(jnp.broadcast_to(block[None], (count,) + block.shape), axis, groups)


def local_softmax(logits, axis):
    high = jnp.max(logits, axis=axis, keepdims=True)
    powers = jnp.exp(logits - high)
    total = jnp.sum(powers, axis=axis)
    mean = jnp.sum(powers * logits, axis=axis) / total
    return jnp.squeeze(high, axis) + jnp.log(total), mean


def merge(norms):
    high = jnp.max(norms, axis=0)
    return high + jnp.log(jnp.sum(jnp.exp(norms - high), axis=0))


def per_device(images, texts, positive, scale_logarithm):
    n_img, n_txt = lax.axis_size("img"), lax.axis_size("txt")
    rows, cols = images.shape[0], texts.shape[0]
    width = images.shape[1] * n_txt
    scale = jnp.exp(scale_logarithm[0])

    text_full = lax.all_gather(texts, "img", axis=1, tiled=True)
    def gather(block):
        by_pair = collect(block, "txt", Y_PAIRS, PAIRS)
        return collect(by_pair, "txt", 2 * X_CHIPS, SQUARES)

    def none(block):
        return jnp.zeros((2 * X_CHIPS, Y_PAIRS) + block.shape, block.dtype)

    by_square = lax.cond(scale > 0, gather, none, images.T)
    image_t = by_square.reshape(X_CHIPS, 2, Y_PAIRS, -1, rows).swapaxes(1, 2).reshape(width, rows)

    logits = scale * lax.dot_general(
        image_t, text_full, (((0,), (1,)), ((), ())), preferred_element_type=jnp.float32
    )
    column_ids = lax.axis_index("txt") * cols + jnp.arange(cols, dtype=jnp.int32)
    matched = (positive[:, None] == column_ids[None, :]).astype(jnp.float32)

    col_norm, col_mean = local_softmax(logits, 0)
    row_norm, row_mean = local_softmax(logits, 1)
    matched_sum = jnp.sum(matched * logits)

    seen = collect(row_norm[None], "txt", n_txt)[:, 0]
    row_norms = merge(seen)
    row_slope = jnp.sum(jnp.exp(row_norm - row_norms) * row_mean)

    packed = jnp.concatenate(
        [
            col_norm,
            col_mean,
            jnp.full((128,), 0.5 * jnp.sum(row_norms)),
            jnp.full((128,), 0.5 * row_slope - matched_sum),
            jnp.full((128,), matched_sum),
        ]
    )
    seen = collect(packed[None], "img", n_img)[:, 0]
    column_norms = merge(seen[:, :cols])
    col_slope = jnp.sum(jnp.exp(seen[:, :cols] - column_norms) * seen[:, cols : 2 * cols])
    row_loss_all = jnp.sum(seen[:, 2 * cols])
    slope_here = 0.5 * col_slope + jnp.sum(seen[:, 2 * cols + 128])
    loss_here = 0.5 * jnp.sum(column_norms) - jnp.sum(seen[:, 2 * cols + 256])

    packed = jnp.concatenate([jnp.full((128,), loss_here), jnp.full((128,), slope_here)])
    seen = collect(packed[None], "txt", n_txt)[:, 0]
    batch = rows * n_img
    loss = ((jnp.sum(seen[:, 0]) + row_loss_all) / batch).reshape(1)
    grad_log_scale = (jnp.sum(seen[:, 128]) / batch).reshape(1)

    weights = (
        0.5 * (jnp.exp(logits - row_norms[:, None]) + jnp.exp(logits - column_norms[None, :]))
        - matched
    ).astype(jnp.bfloat16)

    text_part = scale * lax.dot_general(
        image_t, weights, (((1,), (0,)), ((), ())), preferred_element_type=jnp.float32
    )
    text_part = text_part.astype(jnp.bfloat16).reshape(8, CORES, -1, cols).swapaxes(0, 1)
    text_part = jnp.sum(exchange(text_part, "img", BOTH_CORES).astype(jnp.float32), axis=0)
    grad_texts = lax.psum_scatter(
        text_part.astype(jnp.bfloat16).reshape(-1, cols),
        "img",
        scatter_dimension=0,
        axis_index_groups=ALONG_Z,
        tiled=True,
    ).T

    text_t = text_full.T.reshape(X_CHIPS, Y_PAIRS, 2, -1, cols).swapaxes(1, 2).reshape(width, cols)
    image_part = scale * lax.dot_general(
        text_t, weights, (((1,), (1,)), ((), ())), preferred_element_type=jnp.float32
    )
    image_part = image_part.astype(jnp.bfloat16).reshape(2 * X_CHIPS, -1, rows)
    partial = jnp.sum(exchange(image_part, "txt", SQUARES).astype(jnp.float32), axis=0)
    partial = partial.astype(jnp.bfloat16).reshape(Y_PAIRS, -1, rows)
    partial = jnp.sum(exchange(partial, "txt", PAIRS).astype(jnp.float32), axis=0)
    grad_images = partial.astype(jnp.bfloat16).T
    return (loss, grad_images, grad_texts, grad_log_scale)


def solution(mesh):
    return jax.shard_map(
        per_device,
        mesh=mesh,
        in_specs=(P("img", "txt"), P("txt", "img"), P("img"), P()),
        out_specs=(P(), P("img", "txt"), P("txt", "img"), P()),
        check_vma=False,
    )
```

```python
import jax
import jax.numpy as jnp
from jax import lax
from jax.experimental import pallas as pl
from jax.experimental.pallas import tpu as pltpu
from jax.sharding import PartitionSpec as P

X_CHIPS = 4
Y_PAIRS = 4
Z_CHIPS = 8
CORES = 2
SQUARE = 2 * X_CHIPS
PAIRS = [
    [(x * Y_PAIRS + pair) * 2 + side for pair in range(Y_PAIRS)]
    for x in range(X_CHIPS)
    for side in range(2)
]
SQUARES = [
    [(x * Y_PAIRS + pair) * 2 + side for x in range(X_CHIPS) for side in range(2)]
    for pair in range(Y_PAIRS)
]
BOTH_CORES = [[z * CORES + core for core in range(CORES)] for z in range(Z_CHIPS)]
ALONG_Z = [[z * CORES + core for z in range(Z_CHIPS)] for core in range(CORES)]

LANES = 128
TAIL_ROWS = 8
F32 = jnp.float32
BF16 = jnp.bfloat16


def exchange(blocks, axis, groups=None):
    return lax.all_to_all(blocks, axis, 0, 0, axis_index_groups=groups)


def collect(block, axis, count, groups=None):
    return exchange(jnp.broadcast_to(block[None], (count,) + block.shape), axis, groups)


def vmem():
    return pl.BlockSpec(memory_space=pltpu.VMEM)


def smem():
    return pl.BlockSpec(memory_space=pltpu.SMEM)


def call(kernel, name, in_specs, outs, flops, moved, powers=0, scratch=()):
    out_shape = [jax.ShapeDtypeStruct(shape, dtype) for shape, dtype, _ in outs]
    return pl.pallas_call(
        kernel,
        name=name,
        out_shape=out_shape,
        in_specs=in_specs,
        out_specs=[spec for _, _, spec in outs],
        scratch_shapes=list(scratch),
        compiler_params=pltpu.CompilerParams(vmem_limit_bytes=40 << 20),
        cost_estimate=pl.CostEstimate(flops=flops, bytes_accessed=moved, transcendentals=powers),
    )


def to_lanes(column):
    return jnp.broadcast_to(column, (LANES, LANES)).T[:1]


def to_sublanes(line):
    return jnp.broadcast_to(line, (LANES, LANES)).T[:, :1]


def pick(shape, axis, values):
    index = lax.broadcasted_iota(jnp.int32, shape, axis)
    out = jnp.zeros(shape, F32)
    for k, value in enumerate(values):
        out = jnp.where(index == k, value, out)
    return out


def thirds(value):
    first = value.astype(BF16).astype(F32)
    rest = value - first
    second = rest.astype(BF16).astype(F32)
    return [first, second, (rest - second).astype(BF16).astype(F32)]


def is_match(pos_ref, base_ref, start, rows):
    ids = lax.broadcasted_iota(jnp.int32, (LANES, rows), 0) + (base_ref[0] + start)
    return pos_ref[...] == ids


def tile_kernel(
    scale_ref, base_ref, pos_ref, image_ref, text_ref,
    logit_ref, text_out, row_out, row_norm, row_mean, col_norm, col_mean, matched_out,
):
    depth, cols = text_ref.shape
    rows = pos_ref.shape[1]
    part = depth // (SQUARE * Y_PAIRS)
    for x in range(X_CHIPS):
        for side in range(2):
            for pair in range(Y_PAIRS):
                source = ((x * Y_PAIRS + pair) * 2 + side) * part
                target = ((x * 2 + side) * Y_PAIRS + pair) * part
                text_out[target : target + part, :] = text_ref[source : source + part, :]
    image_t = image_ref[...].reshape(depth, rows)
    row_high = jnp.full((1, rows), -jnp.inf, F32)
    matched = jnp.zeros((1, rows), F32)
    for start in range(0, cols, LANES):
        span = slice(start, start + LANES)
        logits = scale_ref[0] * lax.dot_general(
            text_out[:, span], image_t, (((0,), (0,)), ((), ())), preferred_element_type=F32
        )
        logit_ref[span, :] = logits
        high = jnp.max(logits, axis=1, keepdims=True)
        powers = jnp.exp(logits - high)
        total = jnp.sum(powers, axis=1, keepdims=True)
        mean = jnp.sum(powers * logits, axis=1, keepdims=True) / total
        col_norm[:, span] = to_lanes(high + jnp.log(total))
        col_mean[:, span] = to_lanes(mean)
        row_high = jnp.maximum(row_high, jnp.max(logits, axis=0, keepdims=True))
        mask = is_match(pos_ref, base_ref, start, rows)
        matched += jnp.sum(jnp.where(mask, logits, 0.0), axis=0, keepdims=True)
    total = jnp.zeros((1, rows), F32)
    mean = jnp.zeros((1, rows), F32)
    for start in range(0, cols, LANES):
        logits = logit_ref[start : start + LANES, :]
        powers = jnp.exp(logits - row_high)
        total += jnp.sum(powers, axis=0, keepdims=True)
        mean += jnp.sum(powers * logits, axis=0, keepdims=True)
    norm = row_high + jnp.log(total)
    row_norm[...] = norm
    row_mean[...] = mean / total
    for k in range(row_out.shape[0]):
        row_out[k] = norm
    matched_out[...] = jnp.broadcast_to(jnp.sum(matched, axis=1, keepdims=True), (1, LANES))


def merge(norms):
    high = jnp.max(norms, axis=0, keepdims=True)
    return high + jnp.log(jnp.sum(jnp.exp(norms - high), axis=0, keepdims=True))


def rows_kernel(seen_ref, row_norm, row_mean, col_norm, col_mean, matched_ref, norm_out, col_out):
    norms = merge(seen_ref[:, 0, :])
    norm_out[...] = norms
    slope = jnp.sum(jnp.exp(row_norm[...] - norms) * row_mean[...], axis=1, keepdims=True)
    matched = matched_ref[:, :1]
    sums = [0.5 * jnp.sum(norms, axis=1, keepdims=True), 0.5 * slope - matched, matched]
    sums = pick((1, LANES), 1, sums)
    cols = col_norm.shape[1]
    for k in range(col_out.shape[0]):
        col_out[k, :, :cols] = col_norm[...]
        col_out[k, :, cols : 2 * cols] = col_mean[...]
        col_out[k, :, 2 * cols :] = sums


def weights_kernel(
    parts, scale_ref, base_ref, pos_ref, seen_ref, norm_ref, logit_ref, image_ref,
    weight_out, text_out, sums_out,
):
    cols, rows = logit_ref.shape
    seen = seen_ref[:, 0, :cols]
    norms = merge(seen)
    slope = jnp.sum(jnp.exp(seen - norms) * seen_ref[:, 0, cols : 2 * cols], keepdims=True)
    sums = jnp.sum(seen_ref[:, 0, 2 * cols :], axis=0, keepdims=True)
    loss = 0.5 * jnp.sum(norms, axis=1, keepdims=True) - sums[:, 2:3] + sums[:, :1] / parts
    sums_out[...] = pick((1, LANES), 1, [loss, 0.5 * slope + sums[:, 1:2]])
    row_norms = norm_ref[...]
    for start in range(0, cols, LANES):
        span = slice(start, start + LANES)
        logits = logit_ref[span, :]
        col_norms = to_sublanes(norms[:, span])
        weights = 0.5 * (jnp.exp(logits - row_norms) + jnp.exp(logits - col_norms))
        mask = is_match(pos_ref, base_ref, start, rows)
        weight_out[span, :] = jnp.where(mask, weights - 1.0, weights).astype(BF16)
    weights = weight_out[...]
    part = image_ref.shape[2]
    step = 4
    for first in range(0, SQUARE, step):
        images = image_ref[first : first + step].reshape(step * Y_PAIRS * part, rows)
        grad = scale_ref[0] * lax.dot_general(
            images, weights, (((1,), (1,)), ((), ())), preferred_element_type=F32
        )
        grad = grad.astype(BF16)
        for k in range(step):
            x, side = divmod(first + k, 2)
            for pair in range(Y_PAIRS):
                z, core = divmod(x * Y_PAIRS + pair, CORES)
                at = (k * Y_PAIRS + pair) * part
                text_out[core, z, side * part : (side + 1) * part, :] = grad[at : at + part, :]


def image_kernel(scale_ref, text_ref, weight_ref, sums_ref, out_ref):
    rows = out_ref.shape[2]
    height = text_ref.shape[0] // SQUARE
    weights = weight_ref[...]
    step = 4
    for first in range(0, SQUARE, step):
        grad = scale_ref[0] * jnp.dot(
            text_ref[first * height : (first + step) * height, :], weights,
            preferred_element_type=F32,
        )
        grad = grad.astype(BF16)
        for k in range(step):
            out_ref[first + k, :height, :] = grad[k * height : (k + 1) * height, :]
    pieces = thirds(sums_ref[:, :1]) + thirds(sums_ref[:, 1:2])
    tail = pick((TAIL_ROWS, rows), 0, pieces).astype(BF16)
    for k in range(SQUARE):
        out_ref[k, height:, :] = tail


def square_kernel(seen_ref, out_ref):
    height = seen_ref.shape[1] - TAIL_ROWS
    rows = seen_ref.shape[2]
    part = height // Y_PAIRS
    tail = jnp.sum(seen_ref[:, height:, :LANES].astype(F32), axis=0)
    loss = tail[0:1, :1] + tail[1:2, :1] + tail[2:3, :1]
    slope = tail[3:4, :1] + tail[4:5, :1] + tail[5:6, :1]
    tail = pick((part, LANES), 0, thirds(loss) + thirds(slope)).astype(BF16)
    for pair in range(Y_PAIRS):
        total = jnp.sum(seen_ref[:, pair * part : (pair + 1) * part, :].astype(F32), axis=0)
        out_ref[pair, :, :rows] = total.astype(BF16)
        out_ref[pair, :, rows:] = tail


def pair_kernel(batch, seen_ref, loss_ref, grad_ref, slope_ref):
    rows = grad_ref.shape[1]
    grad_ref[...] = jnp.sum(seen_ref[:, :, :rows].astype(F32), axis=0).astype(BF16)
    tail = jnp.sum(seen_ref[:, :, rows:].astype(F32), axis=0)
    loss_ref[0] = jnp.sum(tail[0:3, :1]) / batch
    slope_ref[0] = jnp.sum(tail[3:6, :1]) / batch


def per_device(images, texts, positive, scale_logarithm):
    n_img, n_txt = lax.axis_size("img"), lax.axis_size("txt")
    rows, cols = images.shape[0], texts.shape[0]
    part = images.shape[1]
    depth = part * n_txt
    batch = rows * n_img
    height = depth // SQUARE
    scale = jnp.exp(scale_logarithm)
    base = (lax.axis_index("txt") * cols).astype(jnp.int32).reshape(1)
    places = positive.reshape(1, rows)

    text_full = lax.all_gather(texts.T, "img", axis=0, tiled=True)

    def gather(block):
        by_pair = collect(block, "txt", Y_PAIRS, PAIRS)
        return collect(by_pair, "txt", SQUARE, SQUARES)

    def none(block):
        return jnp.zeros((SQUARE, Y_PAIRS) + block.shape, block.dtype)

    image_full = lax.cond(scale[0] > 0, gather, none, images.T)

    macs = rows * cols * depth
    logits, text_t, row_out, row_norm, row_mean, col_norm, col_mean, matched = call(
        lambda *refs: tile_kernel(*refs),
        "tile",
        [smem(), smem(), vmem(), vmem(), vmem()],
        [
            ((cols, rows), F32, vmem()),
            ((depth, cols), BF16, vmem()),
            ((n_txt, 1, rows), F32, vmem()),
            ((1, rows), F32, vmem()),
            ((1, rows), F32, vmem()),
            ((1, cols), F32, vmem()),
            ((1, cols), F32, vmem()),
            ((1, LANES), F32, vmem()),
        ],
        2 * macs, 6 << 20, 2 * rows * cols,
    )(scale, base, places, image_full, text_full)

    seen = exchange(row_out, "txt")
    row_norms, col_out = call(
        lambda *refs: rows_kernel(*refs),
        "rows",
        [vmem()] * 6,
        [((1, rows), F32, vmem()), ((n_img, 1, 2 * cols + LANES), F32, vmem())],
        8 * n_txt * rows, 1 << 18, n_txt * rows,
    )(seen, row_norm, row_mean, col_norm, col_mean, matched)

    seen = exchange(col_out, "img")
    weights, text_part, sums = call(
        lambda *refs: weights_kernel(n_txt, *refs),
        "weights",
        [smem(), smem()] + [vmem()] * 5,
        [
            ((cols, rows), BF16, vmem()),
            ((CORES, Z_CHIPS, depth // n_img, cols), BF16, vmem()),
            ((1, LANES), F32, vmem()),
        ],
        2 * macs, 6 << 20, 2 * rows * cols,
    )(scale, base, places, seen, row_norms, logits, image_full)

    text_part = jnp.sum(exchange(text_part, "img", BOTH_CORES).astype(F32), axis=0)
    grad_texts = lax.psum_scatter(
        text_part.astype(BF16).reshape(-1, cols),
        "img",
        scatter_dimension=0,
        axis_index_groups=ALONG_Z,
        tiled=True,
    ).T

    (image_part,) = call(
        lambda *refs: image_kernel(*refs),
        "image",
        [smem(), vmem(), vmem(), vmem()],
        [((SQUARE, height + TAIL_ROWS, rows), BF16, vmem())],
        2 * macs, 4 << 20,
    )(scale, text_t, weights, sums)
    (partial,) = call(
        lambda *refs: square_kernel(*refs),
        "square",
        [vmem()],
        [((Y_PAIRS, part, rows + LANES), BF16, vmem())],
        depth * rows, 3 << 20,
    )(exchange(image_part, "txt", SQUARES))
    loss, grad_images, grad_log_scale = call(
        lambda *refs: pair_kernel(batch, *refs),
        "pair",
        [vmem()],
        [((1,), F32, smem()), ((part, rows), BF16, vmem()), ((1,), F32, smem())],
        Y_PAIRS * part * rows, 1 << 19,
    )(exchange(partial, "txt", PAIRS))
    return (loss, grad_images.T, grad_texts, grad_log_scale)


def solution(mesh):
    return jax.shard_map(
        per_device,
        mesh=mesh,
        in_specs=(P("img", "txt"), P("txt", "img"), P("img"), P()),
        out_specs=(P(), P("img", "txt"), P("txt", "img"), P()),
        check_vma=False,
    )
```

```python
import jax
import jax.numpy as jnp
from jax import lax
from jax.experimental import pallas as pl
from jax.experimental.pallas import tpu as pltpu
from jax.sharding import PartitionSpec as P

X_CHIPS = 4
Y_PAIRS = 4
Z_CHIPS = 8
CORES = 2
SQUARE = 2 * X_CHIPS
PAIRS = [
    [(x * Y_PAIRS + pair) * 2 + side for pair in range(Y_PAIRS)]
    for x in range(X_CHIPS)
    for side in range(2)
]
SQUARES = [
    [(x * Y_PAIRS + pair) * 2 + side for x in range(X_CHIPS) for side in range(2)]
    for pair in range(Y_PAIRS)
]
BOTH_CORES = [[z * CORES + core for core in range(CORES)] for z in range(Z_CHIPS)]
ALONG_Z = [[z * CORES + core for z in range(Z_CHIPS)] for core in range(CORES)]

LANES = 128
TAIL_ROWS = 8
F32 = jnp.float32
BF16 = jnp.bfloat16


def exchange(blocks, axis, groups=None):
    return lax.all_to_all(blocks, axis, 0, 0, axis_index_groups=groups)


def collect(block, axis, count, groups=None):
    return exchange(jnp.broadcast_to(block[None], (count,) + block.shape), axis, groups)


def vmem():
    return pl.BlockSpec(memory_space=pltpu.VMEM)


def smem():
    return pl.BlockSpec(memory_space=pltpu.SMEM)


def call(kernel, name, in_specs, outs, flops, moved, powers=0, scratch=()):
    out_shape = [jax.ShapeDtypeStruct(shape, dtype) for shape, dtype, _ in outs]
    run = pl.pallas_call(
        kernel,
        name=name,
        out_shape=out_shape,
        in_specs=in_specs,
        out_specs=[spec for _, _, spec in outs],
        scratch_shapes=list(scratch),
        compiler_params=pltpu.CompilerParams(vmem_limit_bytes=24 << 20),
        cost_estimate=pl.CostEstimate(flops=flops, bytes_accessed=moved, transcendentals=powers),
    )
    return lambda *operands: tuple(run(*operands))


def to_lanes(column):
    return jnp.broadcast_to(column, (LANES, LANES)).T[:1]


def to_sublanes(line):
    return jnp.broadcast_to(line, (LANES, LANES)).T[:, :1]


def pick(shape, axis, values):
    index = lax.broadcasted_iota(jnp.int32, shape, axis)
    out = jnp.zeros(shape, F32)
    for k, value in enumerate(values):
        out = jnp.where(index == k, value, out)
    return out


def thirds(value):
    first = value.astype(BF16).astype(F32)
    rest = value - first
    second = rest.astype(BF16).astype(F32)
    return [first, second, (rest - second).astype(BF16).astype(F32)]


def is_match(pos_ref, base_ref, start, rows):
    ids = lax.broadcasted_iota(jnp.int32, (LANES, rows), 0) + (base_ref[0] + start)
    return pos_ref[...] == ids


def tile_kernel(
    scale_ref, base_ref, pos_ref, image_ref, text_ref,
    logit_ref, text_out, row_out, row_norm, row_mean, col_norm, col_mean, matched_out,
):
    depth, cols = text_ref.shape
    rows = pos_ref.shape[1]
    part = depth // (SQUARE * Y_PAIRS)
    for x in range(X_CHIPS):
        for side in range(2):
            for pair in range(Y_PAIRS):
                source = ((x * Y_PAIRS + pair) * 2 + side) * part
                target = ((x * 2 + side) * Y_PAIRS + pair) * part
                text_out[target : target + part, :] = text_ref[source : source + part, :]
    image_t = image_ref[...].reshape(depth, rows)
    row_high = jnp.full((1, rows), -jnp.inf, F32)
    matched = jnp.zeros((1, rows), F32)
    for start in range(0, cols, LANES):
        span = slice(start, start + LANES)
        logits = scale_ref[0] * lax.dot_general(
            text_out[:, span], image_t, (((0,), (0,)), ((), ())), preferred_element_type=F32
        )
        logit_ref[span, :] = logits
        high = jnp.max(logits, axis=1, keepdims=True)
        powers = jnp.exp(logits - high)
        total = jnp.sum(powers, axis=1, keepdims=True)
        mean = jnp.sum(powers * logits, axis=1, keepdims=True) / total
        col_norm[:, span] = to_lanes(high + jnp.log(total))
        col_mean[:, span] = to_lanes(mean)
        row_high = jnp.maximum(row_high, jnp.max(logits, axis=0, keepdims=True))
        mask = is_match(pos_ref, base_ref, start, rows)
        matched += jnp.sum(jnp.where(mask, logits, 0.0), axis=0, keepdims=True)
    total = jnp.zeros((1, rows), F32)
    mean = jnp.zeros((1, rows), F32)
    for start in range(0, cols, LANES):
        logits = logit_ref[start : start + LANES, :]
        powers = jnp.exp(logits - row_high)
        total += jnp.sum(powers, axis=0, keepdims=True)
        mean += jnp.sum(powers * logits, axis=0, keepdims=True)
    norm = row_high + jnp.log(total)
    row_norm[...] = norm
    row_mean[...] = mean / total
    for k in range(row_out.shape[0]):
        row_out[k] = norm
    matched_out[...] = jnp.broadcast_to(jnp.sum(matched, axis=1, keepdims=True), (1, LANES))


def merge(norms):
    high = jnp.max(norms, axis=0, keepdims=True)
    return high + jnp.log(jnp.sum(jnp.exp(norms - high), axis=0, keepdims=True))


def rows_kernel(seen_ref, row_norm, row_mean, col_norm, col_mean, matched_ref, norm_out, col_out):
    norms = merge(seen_ref[:, 0, :])
    norm_out[...] = norms
    slope = jnp.sum(jnp.exp(row_norm[...] - norms) * row_mean[...], axis=1, keepdims=True)
    matched = matched_ref[:, :1]
    sums = [0.5 * jnp.sum(norms, axis=1, keepdims=True), 0.5 * slope - matched, matched]
    sums = pick((1, LANES), 1, sums)
    cols = col_norm.shape[1]
    for k in range(col_out.shape[0]):
        col_out[k, :, :cols] = col_norm[...]
        col_out[k, :, cols : 2 * cols] = col_mean[...]
        col_out[k, :, 2 * cols :] = sums


def weights_kernel(
    parts, scale_ref, base_ref, pos_ref, seen_ref, norm_ref, logit_ref, image_ref,
    weight_out, text_out, sums_out,
):
    cols, rows = logit_ref.shape
    seen = seen_ref[:, 0, :cols]
    norms = merge(seen)
    slope = jnp.sum(jnp.exp(seen - norms) * seen_ref[:, 0, cols : 2 * cols], keepdims=True)
    sums = jnp.sum(seen_ref[:, 0, 2 * cols :], axis=0, keepdims=True)
    loss = 0.5 * jnp.sum(norms, axis=1, keepdims=True) - sums[:, 2:3] + sums[:, :1] / parts
    sums_out[...] = pick((1, LANES), 1, [loss, 0.5 * slope + sums[:, 1:2]])
    row_norms = norm_ref[...]
    for start in range(0, cols, LANES):
        span = slice(start, start + LANES)
        logits = logit_ref[span, :]
        col_norms = to_sublanes(norms[:, span])
        weights = 0.5 * (jnp.exp(logits - row_norms) + jnp.exp(logits - col_norms))
        mask = is_match(pos_ref, base_ref, start, rows)
        weight_out[span, :] = jnp.where(mask, weights - 1.0, weights).astype(BF16)
    weights = weight_out[...]
    part = image_ref.shape[2]
    step = 4
    for first in range(0, SQUARE, step):
        images = image_ref[first : first + step].reshape(step * Y_PAIRS * part, rows)
        grad = scale_ref[0] * lax.dot_general(
            images, weights, (((1,), (1,)), ((), ())), preferred_element_type=F32
        )
        grad = grad.astype(BF16)
        for k in range(step):
            x, side = divmod(first + k, 2)
            for pair in range(Y_PAIRS):
                z, core = divmod(x * Y_PAIRS + pair, CORES)
                at = (k * Y_PAIRS + pair) * part
                text_out[core, z, side * part : (side + 1) * part, :] = grad[at : at + part, :]


def image_kernel(scale_ref, text_ref, weight_ref, sums_ref, out_ref):
    rows = out_ref.shape[2]
    height = text_ref.shape[0] // SQUARE
    weights = weight_ref[...]
    step = 4
    for first in range(0, SQUARE, step):
        grad = scale_ref[0] * jnp.dot(
            text_ref[first * height : (first + step) * height, :], weights,
            preferred_element_type=F32,
        )
        grad = grad.astype(BF16)
        for k in range(step):
            out_ref[first + k, :height, :] = grad[k * height : (k + 1) * height, :]
    pieces = thirds(sums_ref[:, :1]) + thirds(sums_ref[:, 1:2])
    tail = pick((TAIL_ROWS, rows), 0, pieces).astype(BF16)
    for k in range(SQUARE):
        out_ref[k, height:, :] = tail


def square_kernel(seen_ref, out_ref):
    height = seen_ref.shape[1] - TAIL_ROWS
    rows = seen_ref.shape[2]
    part = height // Y_PAIRS
    tail = jnp.sum(seen_ref[:, height:, :LANES].astype(F32), axis=0)
    loss = tail[0:1, :1] + tail[1:2, :1] + tail[2:3, :1]
    slope = tail[3:4, :1] + tail[4:5, :1] + tail[5:6, :1]
    tail = pick((part, LANES), 0, thirds(loss) + thirds(slope)).astype(BF16)
    for pair in range(Y_PAIRS):
        total = jnp.sum(seen_ref[:, pair * part : (pair + 1) * part, :].astype(F32), axis=0)
        out_ref[pair, :, :rows] = total.astype(BF16)
        out_ref[pair, :, rows:] = tail


def pair_kernel(batch, seen_ref, loss_ref, grad_ref, slope_ref):
    rows = grad_ref.shape[1]
    grad_ref[...] = jnp.sum(seen_ref[:, :, :rows].astype(F32), axis=0).astype(BF16)
    tail = jnp.sum(seen_ref[:, :, rows:].astype(F32), axis=0)
    loss_ref[0] = jnp.sum(tail[0:3, :1]) / batch
    slope_ref[0] = jnp.sum(tail[3:6, :1]) / batch


def per_device(images, texts, positive, scale_logarithm):
    n_img, n_txt = lax.axis_size("img"), lax.axis_size("txt")
    rows, cols = images.shape[0], texts.shape[0]
    part = images.shape[1]
    depth = part * n_txt
    batch = rows * n_img
    height = depth // SQUARE
    scale = jnp.exp(scale_logarithm)
    base = (lax.axis_index("txt") * cols).astype(jnp.int32).reshape(1)
    places = positive.reshape(1, rows)

    text_full = lax.all_gather(texts.T, "img", axis=0, tiled=True)

    def gather(block):
        by_pair = collect(block, "txt", Y_PAIRS, PAIRS)
        return collect(by_pair, "txt", SQUARE, SQUARES)

    def none(block):
        return jnp.zeros((SQUARE, Y_PAIRS) + block.shape, block.dtype)

    always = scale[0] > -1.0
    image_full = lax.cond(always, gather, none, images.T)

    macs = rows * cols * depth
    logits, text_t, row_out, row_norm, row_mean, col_norm, col_mean, matched = call(
        lambda *refs: tile_kernel(*refs),
        "tile",
        [smem(), smem(), vmem(), vmem(), vmem()],
        [
            ((cols, rows), F32, vmem()),
            ((depth, cols), BF16, vmem()),
            ((n_txt, 1, rows), F32, vmem()),
            ((1, rows), F32, vmem()),
            ((1, rows), F32, vmem()),
            ((1, cols), F32, vmem()),
            ((1, cols), F32, vmem()),
            ((1, LANES), F32, vmem()),
        ],
        2 * macs, 6 << 20, 2 * rows * cols,
    )(scale, base, places, image_full, text_full)

    seen = exchange(row_out, "txt")
    row_norms, col_out = call(
        lambda *refs: rows_kernel(*refs),
        "rows",
        [vmem()] * 6,
        [((1, rows), F32, vmem()), ((n_img, 1, 2 * cols + LANES), F32, vmem())],
        8 * n_txt * rows, 1 << 18, n_txt * rows,
    )(seen, row_norm, row_mean, col_norm, col_mean, matched)

    seen = exchange(col_out, "img")
    weights, text_part, sums = call(
        lambda *refs: weights_kernel(n_txt, *refs),
        "weights",
        [smem(), smem()] + [vmem()] * 5,
        [
            ((cols, rows), BF16, vmem()),
            ((CORES, Z_CHIPS, depth // n_img, cols), BF16, vmem()),
            ((1, LANES), F32, vmem()),
        ],
        2 * macs, 6 << 20, 2 * rows * cols,
    )(scale, base, places, seen, row_norms, logits, image_full)

    text_part = jnp.sum(exchange(text_part, "img", BOTH_CORES).astype(F32), axis=0)
    grad_texts = lax.psum_scatter(
        text_part.astype(BF16).reshape(-1, cols),
        "img",
        scatter_dimension=0,
        axis_index_groups=ALONG_Z,
        tiled=True,
    ).T

    (image_part,) = call(
        lambda *refs: image_kernel(*refs),
        "image",
        [smem(), vmem(), vmem(), vmem()],
        [((SQUARE, height + TAIL_ROWS, rows), BF16, vmem())],
        2 * macs, 4 << 20,
    )(scale, text_t, weights, sums)

    def scatter(image_part):
        (partial,) = call(
            lambda *refs: square_kernel(*refs),
            "square",
            [vmem()],
            [((Y_PAIRS, part, rows + LANES), BF16, vmem())],
            depth * rows, 3 << 20,
        )(exchange(image_part, "txt", SQUARES))
        return call(
            lambda *refs: pair_kernel(batch, *refs),
            "pair",
            [vmem()],
            [((1,), F32, smem()), ((part, rows), BF16, vmem()), ((1,), F32, smem())],
            Y_PAIRS * part * rows, 1 << 19,
        )(exchange(partial, "txt", PAIRS))

    def nothing(image_part):
        return jnp.zeros((1,), F32), jnp.zeros((part, rows), BF16), jnp.zeros((1,), F32)

    loss, grad_images, grad_log_scale = lax.cond(always, scatter, nothing, image_part)
    return (loss, grad_images.T, grad_texts, grad_log_scale)


def solution(mesh):
    return jax.shard_map(
        per_device,
        mesh=mesh,
        in_specs=(P("img", "txt"), P("txt", "img"), P("img"), P()),
        out_specs=(P(), P("img", "txt"), P("txt", "img"), P()),
        check_vma=False,
    )
```

```python
import jax
import jax.numpy as jnp
from jax import lax
from jax.experimental import pallas as pl
from jax.experimental.pallas import tpu as pltpu
from jax.sharding import PartitionSpec as P

X_CHIPS = 4
Y_PAIRS = 4
Z_CHIPS = 8
CORES = 2
SQUARE = 2 * X_CHIPS
PAIRS = [
    [(x * Y_PAIRS + pair) * 2 + side for pair in range(Y_PAIRS)]
    for x in range(X_CHIPS)
    for side in range(2)
]
SQUARES = [
    [(x * Y_PAIRS + pair) * 2 + side for x in range(X_CHIPS) for side in range(2)]
    for pair in range(Y_PAIRS)
]
BOTH_CORES = [[z * CORES + core for core in range(CORES)] for z in range(Z_CHIPS)]
ALONG_Z = [[z * CORES + core for z in range(Z_CHIPS)] for core in range(CORES)]

LANES = 128
TAIL_ROWS = 8
F32 = jnp.float32
BF16 = jnp.bfloat16


def exchange(blocks, axis, groups=None):
    return lax.all_to_all(blocks, axis, 0, 0, axis_index_groups=groups)


def collect(block, axis, count, groups=None):
    return exchange(jnp.broadcast_to(block[None], (count,) + block.shape), axis, groups)


def vmem():
    return pl.BlockSpec(memory_space=pltpu.VMEM)


def smem():
    return pl.BlockSpec(memory_space=pltpu.SMEM)


def call(kernel, name, in_specs, outs, flops, moved, powers=0, scratch=()):
    out_shape = [jax.ShapeDtypeStruct(shape, dtype) for shape, dtype, _ in outs]
    run = pl.pallas_call(
        kernel,
        name=name,
        out_shape=out_shape,
        in_specs=in_specs,
        out_specs=[spec for _, _, spec in outs],
        scratch_shapes=list(scratch),
        compiler_params=pltpu.CompilerParams(vmem_limit_bytes=24 << 20),
        cost_estimate=pl.CostEstimate(flops=flops, bytes_accessed=moved, transcendentals=powers),
    )
    return lambda *operands: tuple(run(*operands))


def to_lanes(column):
    return jnp.broadcast_to(column, (LANES, LANES)).T[:1]


def to_sublanes(line):
    return jnp.broadcast_to(line, (LANES, LANES)).T[:, :1]


def pick(shape, axis, values):
    index = lax.broadcasted_iota(jnp.int32, shape, axis)
    out = jnp.zeros(shape, F32)
    for k, value in enumerate(values):
        out = jnp.where(index == k, value, out)
    return out


def thirds(value):
    first = value.astype(BF16).astype(F32)
    rest = value - first
    second = rest.astype(BF16).astype(F32)
    return [first, second, (rest - second).astype(BF16).astype(F32)]


def is_match(pos_ref, base_ref, start, rows):
    ids = lax.broadcasted_iota(jnp.int32, (LANES, rows), 0) + (base_ref[0] + start)
    return pos_ref[...] == ids


def tile_kernel(
    scale_ref, base_ref, pos_ref, image_ref, text_ref,
    logit_ref, text_out, row_out, row_norm, row_mean, col_norm, col_mean, matched_out,
):
    depth, cols = text_ref.shape
    rows = pos_ref.shape[1]
    part = depth // (SQUARE * Y_PAIRS)
    for x in range(X_CHIPS):
        for side in range(2):
            for pair in range(Y_PAIRS):
                source = ((x * Y_PAIRS + pair) * 2 + side) * part
                target = ((x * 2 + side) * Y_PAIRS + pair) * part
                text_out[target : target + part, :] = text_ref[source : source + part, :]
    image_t = image_ref[...].reshape(depth, rows)
    row_high = jnp.full((1, rows), -jnp.inf, F32)
    matched = jnp.zeros((1, rows), F32)
    for start in range(0, cols, LANES):
        span = slice(start, start + LANES)
        logits = scale_ref[0] * lax.dot_general(
            text_out[:, span], image_t, (((0,), (0,)), ((), ())), preferred_element_type=F32
        )
        logit_ref[span, :] = logits
        high = jnp.max(logits, axis=1, keepdims=True)
        powers = jnp.exp(logits - high)
        total = jnp.sum(powers, axis=1, keepdims=True)
        mean = jnp.sum(powers * logits, axis=1, keepdims=True) / total
        col_norm[:, span] = to_lanes(high + jnp.log(total))
        col_mean[:, span] = to_lanes(mean)
        row_high = jnp.maximum(row_high, jnp.max(logits, axis=0, keepdims=True))
        mask = is_match(pos_ref, base_ref, start, rows)
        matched += jnp.sum(jnp.where(mask, logits, 0.0), axis=0, keepdims=True)
    total = jnp.zeros((1, rows), F32)
    mean = jnp.zeros((1, rows), F32)
    for start in range(0, cols, LANES):
        logits = logit_ref[start : start + LANES, :]
        powers = jnp.exp(logits - row_high)
        total += jnp.sum(powers, axis=0, keepdims=True)
        mean += jnp.sum(powers * logits, axis=0, keepdims=True)
    norm = row_high + jnp.log(total)
    row_norm[...] = norm
    row_mean[...] = mean / total
    for k in range(row_out.shape[0]):
        row_out[k] = norm
    matched_out[...] = jnp.broadcast_to(jnp.sum(matched, axis=1, keepdims=True), (1, LANES))


def merge(norms):
    high = jnp.max(norms, axis=0, keepdims=True)
    return high + jnp.log(jnp.sum(jnp.exp(norms - high), axis=0, keepdims=True))


def rows_kernel(seen_ref, row_norm, row_mean, col_norm, col_mean, matched_ref, norm_out, col_out):
    norms = merge(seen_ref[:, 0, :])
    norm_out[...] = norms
    slope = jnp.sum(jnp.exp(row_norm[...] - norms) * row_mean[...], axis=1, keepdims=True)
    matched = matched_ref[:, :1]
    sums = [0.5 * jnp.sum(norms, axis=1, keepdims=True), 0.5 * slope - matched, matched]
    sums = pick((1, LANES), 1, sums)
    cols = col_norm.shape[1]
    for k in range(col_out.shape[0]):
        col_out[k, :, :cols] = col_norm[...]
        col_out[k, :, cols : 2 * cols] = col_mean[...]
        col_out[k, :, 2 * cols :] = sums


def weights_kernel(
    parts, scale_ref, base_ref, pos_ref, seen_ref, norm_ref, logit_ref, text_ref,
    weight_out, image_out,
):
    cols, rows = logit_ref.shape
    seen = seen_ref[:, 0, :cols]
    norms = merge(seen)
    slope = jnp.sum(jnp.exp(seen - norms) * seen_ref[:, 0, cols : 2 * cols], keepdims=True)
    sums = jnp.sum(seen_ref[:, 0, 2 * cols :], axis=0, keepdims=True)
    loss = 0.5 * jnp.sum(norms, axis=1, keepdims=True) - sums[:, 2:3] + sums[:, :1] / parts
    row_norms = norm_ref[...]
    for start in range(0, cols, LANES):
        span = slice(start, start + LANES)
        logits = logit_ref[span, :]
        col_norms = to_sublanes(norms[:, span])
        weights = 0.5 * (jnp.exp(logits - row_norms) + jnp.exp(logits - col_norms))
        mask = is_match(pos_ref, base_ref, start, rows)
        weight_out[span, :] = jnp.where(mask, weights - 1.0, weights).astype(BF16)
    height = text_ref.shape[0] // SQUARE
    weights = weight_out[...]
    step = 4
    for first in range(0, SQUARE, step):
        grad = scale_ref[0] * jnp.dot(
            text_ref[first * height : (first + step) * height, :], weights,
            preferred_element_type=F32,
        )
        grad = grad.astype(BF16)
        for k in range(step):
            image_out[first + k, :height, :] = grad[k * height : (k + 1) * height, :]
    pieces = thirds(loss) + thirds(0.5 * slope + sums[:, 1:2])
    tail = pick((TAIL_ROWS, rows), 0, pieces).astype(BF16)
    for k in range(SQUARE):
        image_out[k, height:, :] = tail


def text_kernel(scale_ref, core_ref, weight_ref, image_ref, own_out, other_out):
    rows = weight_ref.shape[1]
    weights = weight_ref[...]
    part = image_ref.shape[2]
    mine = core_ref[0] == 0
    step = 4
    for first in range(0, SQUARE, step):
        images = image_ref[first : first + step].reshape(step * Y_PAIRS * part, rows)
        grad = scale_ref[0] * lax.dot_general(
            images, weights, (((1,), (1,)), ((), ())), preferred_element_type=F32
        )
        grad = grad.astype(BF16)
        for k in range(step):
            x, side = divmod(first + k, 2)
            for pair in range(0, Y_PAIRS, CORES):
                z = (x * Y_PAIRS + pair) // CORES
                at = (k * Y_PAIRS + pair) * part
                even, odd = grad[at : at + part, :], grad[at + part : at + 2 * part, :]
                here = slice(side * part, (side + 1) * part)
                own_out[z, here, :] = jnp.where(mine, even, odd)
                other_out[z, here, :] = jnp.where(mine, odd, even)


def square_kernel(seen_ref, out_ref):
    height = seen_ref.shape[1] - TAIL_ROWS
    rows = seen_ref.shape[2]
    part = height // Y_PAIRS
    tail = jnp.sum(seen_ref[:, height:, :LANES].astype(F32), axis=0)
    loss = tail[0:1, :1] + tail[1:2, :1] + tail[2:3, :1]
    slope = tail[3:4, :1] + tail[4:5, :1] + tail[5:6, :1]
    tail = pick((part, LANES), 0, thirds(loss) + thirds(slope)).astype(BF16)
    for pair in range(Y_PAIRS):
        total = jnp.sum(seen_ref[:, pair * part : (pair + 1) * part, :].astype(F32), axis=0)
        out_ref[pair, :, :rows] = total.astype(BF16)
        out_ref[pair, :, rows:] = tail


def pair_kernel(batch, seen_ref, loss_ref, grad_ref, slope_ref):
    rows = grad_ref.shape[1]
    grad_ref[...] = jnp.sum(seen_ref[:, :, :rows].astype(F32), axis=0).astype(BF16)
    tail = jnp.sum(seen_ref[:, :, rows:].astype(F32), axis=0)
    loss_ref[0] = jnp.sum(tail[0:3, :1]) / batch
    slope_ref[0] = jnp.sum(tail[3:6, :1]) / batch


def per_device(images, texts, positive, scale_logarithm):
    n_img, n_txt = lax.axis_size("img"), lax.axis_size("txt")
    rows, cols = images.shape[0], texts.shape[0]
    part = images.shape[1]
    depth = part * n_txt
    batch = rows * n_img
    height = depth // SQUARE
    scale = jnp.exp(scale_logarithm)
    base = (lax.axis_index("txt") * cols).astype(jnp.int32).reshape(1)
    core = (lax.axis_index("img") % CORES).astype(jnp.int32).reshape(1)
    places = positive.reshape(1, rows)

    text_full = lax.all_gather(texts.T, "img", axis=0, tiled=True)

    def gather(block):
        by_pair = collect(block, "txt", Y_PAIRS, PAIRS)
        return collect(by_pair, "txt", SQUARE, SQUARES)

    def none(block):
        return jnp.zeros((SQUARE, Y_PAIRS) + block.shape, block.dtype)

    always = scale[0] > -1.0
    image_full = lax.cond(always, gather, none, images.T)

    macs = rows * cols * depth
    logits, text_t, row_out, row_norm, row_mean, col_norm, col_mean, matched = call(
        lambda *refs: tile_kernel(*refs),
        "tile",
        [smem(), smem(), vmem(), vmem(), vmem()],
        [
            ((cols, rows), F32, vmem()),
            ((depth, cols), BF16, vmem()),
            ((n_txt, 1, rows), F32, vmem()),
            ((1, rows), F32, vmem()),
            ((1, rows), F32, vmem()),
            ((1, cols), F32, vmem()),
            ((1, cols), F32, vmem()),
            ((1, LANES), F32, vmem()),
        ],
        2 * macs, 6 << 20, 2 * rows * cols,
    )(scale, base, places, image_full, text_full)

    seen = exchange(row_out, "txt")
    row_norms, col_out = call(
        lambda *refs: rows_kernel(*refs),
        "rows",
        [vmem()] * 6,
        [((1, rows), F32, vmem()), ((n_img, 1, 2 * cols + LANES), F32, vmem())],
        8 * n_txt * rows, 1 << 18, n_txt * rows,
    )(seen, row_norm, row_mean, col_norm, col_mean, matched)

    seen = exchange(col_out, "img")
    weights, image_part = call(
        lambda *refs: weights_kernel(n_txt, *refs),
        "weights",
        [smem(), smem()] + [vmem()] * 5,
        [((cols, rows), BF16, vmem()), ((SQUARE, height + TAIL_ROWS, rows), BF16, vmem())],
        2 * macs, 6 << 20, 2 * rows * cols,
    )(scale, base, places, seen, row_norms, logits, text_t)

    half = (Z_CHIPS, depth // n_img, cols)
    own, other = call(
        lambda *refs: text_kernel(*refs),
        "texts",
        [smem(), smem(), vmem(), vmem()],
        [(half, BF16, vmem()), (half, BF16, vmem())],
        2 * macs, 4 << 20,
    )(scale, core, weights, image_full)
    swap = [(z * CORES + c, z * CORES + 1 - c) for z in range(Z_CHIPS) for c in range(CORES)]
    text_part = own.astype(F32) + lax.ppermute(other, "img", swap).astype(F32)
    grad_texts = lax.psum_scatter(
        text_part.astype(BF16).reshape(-1, cols),
        "img",
        scatter_dimension=0,
        axis_index_groups=ALONG_Z,
        tiled=True,
    ).T

    (partial,) = call(
        lambda *refs: square_kernel(*refs),
        "square",
        [vmem()],
        [((Y_PAIRS, part, rows + LANES), BF16, vmem())],
        depth * rows, 3 << 20,
    )(exchange(image_part, "txt", SQUARES))
    loss, grad_images, grad_log_scale = call(
        lambda *refs: pair_kernel(batch, *refs),
        "pair",
        [vmem()],
        [((1,), F32, smem()), ((part, rows), BF16, vmem()), ((1,), F32, smem())],
        Y_PAIRS * part * rows, 1 << 19,
    )(exchange(partial, "txt", PAIRS))
    return (loss, grad_images.T, grad_texts, grad_log_scale)


def solution(mesh):
    return jax.shard_map(
        per_device,
        mesh=mesh,
        in_specs=(P("img", "txt"), P("txt", "img"), P("img"), P()),
        out_specs=(P(), P("img", "txt"), P("txt", "img"), P()),
        check_vma=False,
    )
```

```python
import jax
import jax.numpy as jnp
from jax import lax
from jax.experimental import pallas as pl
from jax.experimental.pallas import tpu as pltpu
from jax.sharding import PartitionSpec as P

X_CHIPS = 4
Y_PAIRS = 4
Z_CHIPS = 8
CORES = 2
SQUARE = 2 * X_CHIPS
PAIRS = [
    [(x * Y_PAIRS + pair) * 2 + side for pair in range(Y_PAIRS)]
    for x in range(X_CHIPS)
    for side in range(2)
]
SQUARES = [
    [(x * Y_PAIRS + pair) * 2 + side for x in range(X_CHIPS) for side in range(2)]
    for pair in range(Y_PAIRS)
]
ALONG_Z = [[z * CORES + core for z in range(Z_CHIPS)] for core in range(CORES)]

LANES = 128
TAIL_ROWS = 8
BLOCK = 256
F32 = jnp.float32
BF16 = jnp.bfloat16


def exchange(blocks, axis, groups=None):
    return lax.all_to_all(blocks, axis, 0, 0, axis_index_groups=groups)


def collect(block, axis, count, groups=None):
    return exchange(jnp.broadcast_to(block[None], (count,) + block.shape), axis, groups)


def vmem():
    return pl.BlockSpec(memory_space=pltpu.VMEM)


def hbm():
    return pl.BlockSpec(memory_space=pltpu.HBM)


def smem():
    return pl.BlockSpec(memory_space=pltpu.SMEM)


def call(kernel, name, in_specs, outs, flops, moved, powers=0, scratch=(), limit=48):
    out_shape = [jax.ShapeDtypeStruct(shape, dtype) for shape, dtype, _ in outs]
    run = pl.pallas_call(
        kernel,
        name=name,
        out_shape=out_shape,
        in_specs=in_specs,
        out_specs=[spec for _, _, spec in outs],
        scratch_shapes=list(scratch),
        compiler_params=pltpu.CompilerParams(vmem_limit_bytes=limit << 20),
        cost_estimate=pl.CostEstimate(flops=flops, bytes_accessed=moved, transcendentals=powers),
    )
    return lambda *operands: tuple(run(*operands))


def to_lanes(column):
    return jnp.broadcast_to(column, (LANES, LANES)).T[:1]


def to_sublanes(line):
    return jnp.broadcast_to(line, (LANES, LANES)).T[:, :1]


def pick(shape, axis, values):
    index = lax.broadcasted_iota(jnp.int32, shape, axis)
    out = jnp.zeros(shape, F32)
    for k, value in enumerate(values):
        out = jnp.where(index == k, value, out)
    return out


def thirds(value):
    first = value.astype(BF16).astype(F32)
    rest = value - first
    second = rest.astype(BF16).astype(F32)
    return [first, second, (rest - second).astype(BF16).astype(F32)]


def is_match(pos_ref, base_ref, start, rows):
    ids = lax.broadcasted_iota(jnp.int32, (LANES, rows), 0) + (base_ref[0] + start)
    return pos_ref[...] == ids


def tile_kernel(
    scale_ref, base_ref, pos_ref, image_in, text_ref,
    logit_ref, text_out, row_out, row_norm, row_mean, col_norm, col_mean, matched_out,
    image_ref, image_sems,
):
    depth, cols = text_ref.shape
    rows = pos_ref.shape[1]
    part = depth // (SQUARE * Y_PAIRS)
    reads = []
    for k in range(rows // BLOCK):
        span = pl.ds(k * BLOCK, BLOCK)
        reads.append(
            pltpu.make_async_copy(
                image_in.at[:, :, :, span], image_ref.at[:, :, :, span], image_sems.at[k]
            )
        )
        reads[-1].start()
    for x in range(X_CHIPS):
        for side in range(2):
            for pair in range(Y_PAIRS):
                source = ((x * Y_PAIRS + pair) * 2 + side) * part
                target = ((x * 2 + side) * Y_PAIRS + pair) * part
                text_out[target : target + part, :] = text_ref[source : source + part, :]
    text_t = text_out[...]
    ids = lax.broadcasted_iota(jnp.int32, (cols, BLOCK), 0) + base_ref[0]
    matched = jnp.zeros((1, BLOCK), F32)
    for k, read in enumerate(reads):
        span = slice(k * BLOCK, (k + 1) * BLOCK)
        read.wait()
        logits = scale_ref[0] * lax.dot_general(
            text_t, image_ref[:, :, :, span].reshape(depth, BLOCK), (((0,), (0,)), ((), ())),
            preferred_element_type=F32,
        )
        logit_ref[:, span] = logits
        high = jnp.max(logits, axis=0, keepdims=True)
        powers = jnp.exp(logits - high)
        total = jnp.sum(powers, axis=0, keepdims=True)
        mean = jnp.sum(powers * logits, axis=0, keepdims=True) / total
        row_norm[:, span] = high + jnp.log(total)
        row_mean[:, span] = mean
        mask = pos_ref[:, span] == ids
        matched += jnp.sum(jnp.where(mask, logits, 0.0), axis=0, keepdims=True)
    for start in range(0, cols, LANES):
        span = slice(start, start + LANES)
        logits = logit_ref[span, :]
        high = jnp.max(logits, axis=1, keepdims=True)
        powers = jnp.exp(logits - high)
        total = jnp.sum(powers, axis=1, keepdims=True)
        mean = jnp.sum(powers * logits, axis=1, keepdims=True) / total
        col_norm[:, span] = to_lanes(high + jnp.log(total))
        col_mean[:, span] = to_lanes(mean)
    norm = row_norm[...]
    for k in range(row_out.shape[0]):
        row_out[k] = norm
    matched_out[...] = jnp.broadcast_to(jnp.sum(matched, axis=1, keepdims=True), (1, LANES))


def merge(norms):
    high = jnp.max(norms, axis=0, keepdims=True)
    return high + jnp.log(jnp.sum(jnp.exp(norms - high), axis=0, keepdims=True))


def rows_kernel(seen_ref, row_norm, row_mean, col_norm, col_mean, matched_ref, norm_out, col_out):
    norms = merge(seen_ref[:, 0, :])
    norm_out[...] = norms
    slope = jnp.sum(jnp.exp(row_norm[...] - norms) * row_mean[...], axis=1, keepdims=True)
    matched = matched_ref[:, :1]
    sums = [0.5 * jnp.sum(norms, axis=1, keepdims=True), 0.5 * slope - matched, matched]
    sums = pick((1, LANES), 1, sums)
    cols = col_norm.shape[1]
    for k in range(col_out.shape[0]):
        col_out[k, :, :cols] = col_norm[...]
        col_out[k, :, cols : 2 * cols] = col_mean[...]
        col_out[k, :, 2 * cols :] = sums


def weights_kernel(
    parts, scale_ref, base_ref, pos_ref, seen_ref, norm_ref, logit_ref, text_ref,
    weight_out, image_out, image_ref, image_sems,
):
    cols, rows = logit_ref.shape
    seen = seen_ref[:, 0, :cols]
    norms = merge(seen)
    slope = jnp.sum(jnp.exp(seen - norms) * seen_ref[:, 0, cols : 2 * cols], keepdims=True)
    sums = jnp.sum(seen_ref[:, 0, 2 * cols :], axis=0, keepdims=True)
    loss = 0.5 * jnp.sum(norms, axis=1, keepdims=True) - sums[:, 2:3] + sums[:, :1] / parts
    row_norms = norm_ref[...]
    for start in range(0, cols, LANES):
        span = slice(start, start + LANES)
        logits = logit_ref[span, :]
        col_norms = to_sublanes(norms[:, span])
        weights = 0.5 * (jnp.exp(logits - row_norms) + jnp.exp(logits - col_norms))
        mask = is_match(pos_ref, base_ref, start, rows)
        weight_out[span, :] = jnp.where(mask, weights - 1.0, weights).astype(BF16)
    height = text_ref.shape[0] // SQUARE
    pieces = thirds(loss) + thirds(0.5 * slope + sums[:, 1:2])
    tail = pick((TAIL_ROWS, rows), 0, pieces).astype(BF16)
    for k in range(SQUARE):
        image_ref[k, height:, :] = tail
    weights = weight_out[...]
    step = 2
    copies = []
    for first in range(0, SQUARE, step):
        grad = scale_ref[0] * jnp.dot(
            text_ref[first * height : (first + step) * height, :], weights,
            preferred_element_type=F32,
        )
        grad = grad.astype(BF16)
        for k in range(step):
            image_ref[first + k, :height, :] = grad[k * height : (k + 1) * height, :]
        span = pl.ds(first, step)
        copies.append(
            pltpu.make_async_copy(
                image_ref.at[span], image_out.at[span], image_sems.at[first // step]
            )
        )
        copies[-1].start()
    for copy in copies:
        copy.wait()


def text_kernel(scale_ref, core_ref, weight_ref, image_ref, own_out, other_out):
    rows = weight_ref.shape[1]
    weights = weight_ref[...]
    part = image_ref.shape[2]
    mine = core_ref[0] == 0
    step = 4
    for first in range(0, SQUARE, step):
        images = image_ref[first : first + step].reshape(step * Y_PAIRS * part, rows)
        grad = scale_ref[0] * lax.dot_general(
            images, weights, (((1,), (1,)), ((), ())), preferred_element_type=F32
        )
        grad = grad.astype(BF16)
        for k in range(step):
            x, side = divmod(first + k, 2)
            for pair in range(0, Y_PAIRS, CORES):
                z = (x * Y_PAIRS + pair) // CORES
                at = (k * Y_PAIRS + pair) * part
                even, odd = grad[at : at + part, :], grad[at + part : at + 2 * part, :]
                here = slice(side * part, (side + 1) * part)
                own_out[z, here, :] = jnp.where(mine, even, odd)
                other_out[z, here, :] = jnp.where(mine, odd, even)


def square_kernel(seen_ref, out_ref):
    height = seen_ref.shape[1] - TAIL_ROWS
    rows = seen_ref.shape[2]
    part = height // Y_PAIRS
    tail = jnp.sum(seen_ref[:, height:, :LANES].astype(F32), axis=0)
    loss = tail[0:1, :1] + tail[1:2, :1] + tail[2:3, :1]
    slope = tail[3:4, :1] + tail[4:5, :1] + tail[5:6, :1]
    tail = pick((part, LANES), 0, thirds(loss) + thirds(slope)).astype(BF16)
    for pair in range(Y_PAIRS):
        total = jnp.sum(seen_ref[:, pair * part : (pair + 1) * part, :].astype(F32), axis=0)
        out_ref[pair, :, :rows] = total.astype(BF16)
        out_ref[pair, :, rows:] = tail


def pair_kernel(batch, seen_ref, loss_ref, grad_ref, slope_ref):
    rows = grad_ref.shape[1]
    grad_ref[...] = jnp.sum(seen_ref[:, :, :rows].astype(F32), axis=0).astype(BF16)
    tail = jnp.sum(seen_ref[:, :, rows:].astype(F32), axis=0)
    loss_ref[0] = jnp.sum(tail[0:3, :1]) / batch
    slope_ref[0] = jnp.sum(tail[3:6, :1]) / batch


def per_device(images, texts, positive, scale_logarithm):
    n_img, n_txt = lax.axis_size("img"), lax.axis_size("txt")
    rows, cols = images.shape[0], texts.shape[0]
    part = images.shape[1]
    depth = part * n_txt
    batch = rows * n_img
    height = depth // SQUARE
    scale = jnp.exp(scale_logarithm)
    base = (lax.axis_index("txt") * cols).astype(jnp.int32).reshape(1)
    core = (lax.axis_index("img") % CORES).astype(jnp.int32).reshape(1)
    places = positive.reshape(1, rows)

    text_full = lax.all_gather(texts.T, "img", axis=0, tiled=True)

    def gather(block):
        by_pair = collect(block, "txt", Y_PAIRS, PAIRS)
        return collect(by_pair, "txt", SQUARE, SQUARES)

    def none(block):
        return jnp.zeros((SQUARE, Y_PAIRS) + block.shape, block.dtype)

    always = scale[0] > -1.0
    image_full = lax.cond(always, gather, none, images.T)

    macs = rows * cols * depth
    logits, text_t, row_out, row_norm, row_mean, col_norm, col_mean, matched = call(
        lambda *refs: tile_kernel(*refs),
        "tile",
        [smem(), smem(), vmem(), hbm(), vmem()],
        [
            ((cols, rows), F32, vmem()),
            ((depth, cols), BF16, vmem()),
            ((n_txt, 1, rows), F32, vmem()),
            ((1, rows), F32, vmem()),
            ((1, rows), F32, vmem()),
            ((1, cols), F32, vmem()),
            ((1, cols), F32, vmem()),
            ((1, LANES), F32, vmem()),
        ],
        2 * macs, 6 << 20, 2 * rows * cols,
        [
            pltpu.VMEM(image_full.shape, BF16),
            pltpu.SemaphoreType.DMA((rows // BLOCK,)),
        ],
    )(scale, base, places, image_full, text_full)

    seen = exchange(row_out, "txt")
    row_norms, col_out = call(
        lambda *refs: rows_kernel(*refs),
        "rows",
        [vmem()] * 6,
        [((1, rows), F32, vmem()), ((n_img, 1, 2 * cols + LANES), F32, vmem())],
        8 * n_txt * rows, 1 << 18, n_txt * rows,
    )(seen, row_norm, row_mean, col_norm, col_mean, matched)

    seen = exchange(col_out, "img")
    weights, image_part = call(
        lambda *refs: weights_kernel(n_txt, *refs),
        "weights",
        [smem(), smem()] + [vmem()] * 5,
        [((cols, rows), BF16, vmem()), ((SQUARE, height + TAIL_ROWS, rows), BF16, hbm())],
        2 * macs, 6 << 20, 2 * rows * cols,
        [
            pltpu.VMEM((SQUARE, height + TAIL_ROWS, rows), BF16),
            pltpu.SemaphoreType.DMA((SQUARE // 2,)),
        ],
        48,
    )(scale, base, places, seen, row_norms, logits, text_t)

    half = (Z_CHIPS, depth // n_img, cols)
    own, other = call(
        lambda *refs: text_kernel(*refs),
        "texts",
        [smem(), smem(), vmem(), vmem()],
        [(half, BF16, vmem()), (half, BF16, vmem())],
        2 * macs, 4 << 20,
    )(scale, core, weights, image_full)
    swap = [(z * CORES + c, z * CORES + 1 - c) for z in range(Z_CHIPS) for c in range(CORES)]
    text_part = own.astype(F32) + lax.ppermute(other, "img", swap).astype(F32)
    grad_texts = lax.psum_scatter(
        text_part.astype(BF16).reshape(-1, cols),
        "img",
        scatter_dimension=0,
        axis_index_groups=ALONG_Z,
        tiled=True,
    ).T

    (partial,) = call(
        lambda *refs: square_kernel(*refs),
        "square",
        [vmem()],
        [((Y_PAIRS, part, rows + LANES), BF16, vmem())],
        depth * rows, 3 << 20,
    )(exchange(image_part, "txt", SQUARES))
    loss, grad_images, grad_log_scale = call(
        lambda *refs: pair_kernel(batch, *refs),
        "pair",
        [vmem()],
        [((1,), F32, smem()), ((part, rows), BF16, vmem()), ((1,), F32, smem())],
        Y_PAIRS * part * rows, 1 << 19,
    )(exchange(partial, "txt", PAIRS))
    return (loss, grad_images.T, grad_texts, grad_log_scale)


def solution(mesh):
    return jax.shard_map(
        per_device,
        mesh=mesh,
        in_specs=(P("img", "txt"), P("txt", "img"), P("img"), P()),
        out_specs=(P(), P("img", "txt"), P("txt", "img"), P()),
        check_vma=False,
    )
```

```python
import jax
import jax.numpy as jnp
from jax import lax
from jax.experimental import pallas as pl
from jax.experimental.pallas import tpu as pltpu
from jax.sharding import PartitionSpec as P

X_CHIPS = 4
Y_PAIRS = 4
Z_CHIPS = 8
CORES = 2
SQUARE = 2 * X_CHIPS
PAIRS = [
    [(x * Y_PAIRS + pair) * 2 + side for pair in range(Y_PAIRS)]
    for x in range(X_CHIPS)
    for side in range(2)
]
SQUARES = [
    [(x * Y_PAIRS + pair) * 2 + side for x in range(X_CHIPS) for side in range(2)]
    for pair in range(Y_PAIRS)
]
ALONG_Z = [[z * CORES + core for z in range(Z_CHIPS)] for core in range(CORES)]

LANES = 128
TAIL_ROWS = 8
F32 = jnp.float32
BF16 = jnp.bfloat16


def exchange(blocks, axis, groups=None):
    return lax.all_to_all(blocks, axis, 0, 0, axis_index_groups=groups)


def collect(block, axis, count, groups=None):
    return exchange(jnp.broadcast_to(block[None], (count,) + block.shape), axis, groups)


def vmem():
    return pl.BlockSpec(memory_space=pltpu.VMEM)


def hbm():
    return pl.BlockSpec(memory_space=pltpu.HBM)


def smem():
    return pl.BlockSpec(memory_space=pltpu.SMEM)


def call(kernel, name, in_specs, outs, flops, moved, powers=0, scratch=(), limit=48):
    out_shape = [jax.ShapeDtypeStruct(shape, dtype) for shape, dtype, _ in outs]
    run = pl.pallas_call(
        kernel,
        name=name,
        out_shape=out_shape,
        in_specs=in_specs,
        out_specs=[spec for _, _, spec in outs],
        scratch_shapes=list(scratch),
        compiler_params=pltpu.CompilerParams(vmem_limit_bytes=limit << 20),
        cost_estimate=pl.CostEstimate(flops=flops, bytes_accessed=moved, transcendentals=powers),
    )
    return lambda *operands: tuple(run(*operands))


def to_lanes(column):
    return jnp.broadcast_to(column, (LANES, LANES)).T[:1]


def to_sublanes(line):
    return jnp.broadcast_to(line, (LANES, LANES)).T[:, :1]


def pick(shape, axis, values):
    index = lax.broadcasted_iota(jnp.int32, shape, axis)
    out = jnp.zeros(shape, F32)
    for k, value in enumerate(values):
        out = jnp.where(index == k, value, out)
    return out


def thirds(value):
    first = value.astype(BF16).astype(F32)
    rest = value - first
    second = rest.astype(BF16).astype(F32)
    return [first, second, (rest - second).astype(BF16).astype(F32)]


def is_match(pos_ref, base_ref, start, rows):
    ids = lax.broadcasted_iota(jnp.int32, (LANES, rows), 0) + (base_ref[0] + start)
    return pos_ref[...] == ids


def stay(block):
    return pl.pallas_call(
        lambda block_ref, same_ref: None,
        name="stay",
        out_shape=jax.ShapeDtypeStruct(block.shape, block.dtype),
        in_specs=[hbm()],
        out_specs=hbm(),
        input_output_aliases={0: 0},
        compiler_params=pltpu.CompilerParams(vmem_limit_bytes=57 << 20),
    )(block)


def tile_kernel(
    scale_ref, base_ref, pos_ref, image_ref, text_ref,
    logit_ref, text_out, row_out, row_norm, row_mean, col_norm, col_mean, matched_out,
):
    depth, cols = text_ref.shape
    rows = pos_ref.shape[1]
    part = depth // (SQUARE * Y_PAIRS)
    for x in range(X_CHIPS):
        for side in range(2):
            for pair in range(Y_PAIRS):
                source = ((x * Y_PAIRS + pair) * 2 + side) * part
                target = ((x * 2 + side) * Y_PAIRS + pair) * part
                text_out[target : target + part, :] = text_ref[source : source + part, :]
    image_t = image_ref[...].reshape(depth, rows)
    row_high = jnp.full((1, rows), -jnp.inf, F32)
    matched = jnp.zeros((1, rows), F32)
    for start in range(0, cols, LANES):
        span = slice(start, start + LANES)
        logits = scale_ref[0] * lax.dot_general(
            text_out[:, span], image_t, (((0,), (0,)), ((), ())), preferred_element_type=F32
        )
        logit_ref[span, :] = logits
        high = jnp.max(logits, axis=1, keepdims=True)
        powers = jnp.exp(logits - high)
        total = jnp.sum(powers, axis=1, keepdims=True)
        mean = jnp.sum(powers * logits, axis=1, keepdims=True) / total
        col_norm[:, span] = to_lanes(high + jnp.log(total))
        col_mean[:, span] = to_lanes(mean)
        row_high = jnp.maximum(row_high, jnp.max(logits, axis=0, keepdims=True))
        mask = is_match(pos_ref, base_ref, start, rows)
        matched += jnp.sum(jnp.where(mask, logits, 0.0), axis=0, keepdims=True)
    total = jnp.zeros((1, rows), F32)
    mean = jnp.zeros((1, rows), F32)
    for start in range(0, cols, LANES):
        logits = logit_ref[start : start + LANES, :]
        powers = jnp.exp(logits - row_high)
        total += jnp.sum(powers, axis=0, keepdims=True)
        mean += jnp.sum(powers * logits, axis=0, keepdims=True)
    norm = row_high + jnp.log(total)
    row_norm[...] = norm
    row_mean[...] = mean / total
    for k in range(row_out.shape[0]):
        row_out[k] = norm
    matched_out[...] = jnp.broadcast_to(jnp.sum(matched, axis=1, keepdims=True), (1, LANES))


def merge(norms):
    high = jnp.max(norms, axis=0, keepdims=True)
    return high + jnp.log(jnp.sum(jnp.exp(norms - high), axis=0, keepdims=True))


def rows_kernel(seen_ref, row_norm, row_mean, col_norm, col_mean, matched_ref, norm_out, col_out):
    norms = merge(seen_ref[:, 0, :])
    norm_out[...] = norms
    slope = jnp.sum(jnp.exp(row_norm[...] - norms) * row_mean[...], axis=1, keepdims=True)
    matched = matched_ref[:, :1]
    sums = [0.5 * jnp.sum(norms, axis=1, keepdims=True), 0.5 * slope - matched, matched]
    sums = pick((1, LANES), 1, sums)
    cols = col_norm.shape[1]
    for k in range(col_out.shape[0]):
        col_out[k, :, :cols] = col_norm[...]
        col_out[k, :, cols : 2 * cols] = col_mean[...]
        col_out[k, :, 2 * cols :] = sums


def weights_kernel(
    parts, scale_ref, base_ref, pos_ref, seen_ref, norm_ref, logit_ref, text_ref,
    weight_out, image_out, image_ref, image_sems,
):
    cols, rows = logit_ref.shape
    seen = seen_ref[:, 0, :cols]
    norms = merge(seen)
    slope = jnp.sum(jnp.exp(seen - norms) * seen_ref[:, 0, cols : 2 * cols], keepdims=True)
    sums = jnp.sum(seen_ref[:, 0, 2 * cols :], axis=0, keepdims=True)
    loss = 0.5 * jnp.sum(norms, axis=1, keepdims=True) - sums[:, 2:3] + sums[:, :1] / parts
    row_norms = norm_ref[...]
    for start in range(0, cols, LANES):
        span = slice(start, start + LANES)
        logits = logit_ref[span, :]
        col_norms = to_sublanes(norms[:, span])
        weights = 0.5 * (jnp.exp(logits - row_norms) + jnp.exp(logits - col_norms))
        mask = is_match(pos_ref, base_ref, start, rows)
        weight_out[span, :] = jnp.where(mask, weights - 1.0, weights).astype(BF16)
    height = text_ref.shape[0] // SQUARE
    pieces = thirds(loss) + thirds(0.5 * slope + sums[:, 1:2])
    tail = pick((TAIL_ROWS, rows), 0, pieces).astype(BF16)
    for k in range(SQUARE):
        image_ref[k, height:, :] = tail
    weights = weight_out[...]
    step = 2
    copies = []
    for first in range(0, SQUARE, step):
        grad = scale_ref[0] * jnp.dot(
            text_ref[first * height : (first + step) * height, :], weights,
            preferred_element_type=F32,
        )
        grad = grad.astype(BF16)
        for k in range(step):
            image_ref[first + k, :height, :] = grad[k * height : (k + 1) * height, :]
        span = pl.ds(first, step)
        copies.append(
            pltpu.make_async_copy(
                image_ref.at[span], image_out.at[span], image_sems.at[first // step]
            )
        )
        copies[-1].start()
    for copy in copies:
        copy.wait()


def text_kernel(scale_ref, core_ref, weight_ref, image_ref, own_out, other_out):
    rows = weight_ref.shape[1]
    weights = weight_ref[...]
    part = image_ref.shape[2]
    mine = core_ref[0] == 0
    step = 4
    for first in range(0, SQUARE, step):
        images = image_ref[first : first + step].reshape(step * Y_PAIRS * part, rows)
        grad = scale_ref[0] * lax.dot_general(
            images, weights, (((1,), (1,)), ((), ())), preferred_element_type=F32
        )
        grad = grad.astype(BF16)
        for k in range(step):
            x, side = divmod(first + k, 2)
            for pair in range(0, Y_PAIRS, CORES):
                z = (x * Y_PAIRS + pair) // CORES
                at = (k * Y_PAIRS + pair) * part
                even, odd = grad[at : at + part, :], grad[at + part : at + 2 * part, :]
                here = slice(side * part, (side + 1) * part)
                own_out[z, here, :] = jnp.where(mine, even, odd)
                other_out[z, here, :] = jnp.where(mine, odd, even)


def square_kernel(seen_ref, out_ref):
    height = seen_ref.shape[1] - TAIL_ROWS
    rows = seen_ref.shape[2]
    part = height // Y_PAIRS
    tail = jnp.sum(seen_ref[:, height:, :LANES].astype(F32), axis=0)
    loss = tail[0:1, :1] + tail[1:2, :1] + tail[2:3, :1]
    slope = tail[3:4, :1] + tail[4:5, :1] + tail[5:6, :1]
    tail = pick((part, LANES), 0, thirds(loss) + thirds(slope)).astype(BF16)
    for pair in range(Y_PAIRS):
        total = jnp.sum(seen_ref[:, pair * part : (pair + 1) * part, :].astype(F32), axis=0)
        out_ref[pair, :, :rows] = total.astype(BF16)
        out_ref[pair, :, rows:] = tail


def pair_kernel(batch, seen_ref, loss_ref, grad_ref, slope_ref):
    rows = grad_ref.shape[1]
    grad_ref[...] = jnp.sum(seen_ref[:, :, :rows].astype(F32), axis=0).astype(BF16)
    tail = jnp.sum(seen_ref[:, :, rows:].astype(F32), axis=0)
    loss_ref[0] = jnp.sum(tail[0:3, :1]) / batch
    slope_ref[0] = jnp.sum(tail[3:6, :1]) / batch


def per_device(images, texts, positive, scale_logarithm):
    n_img, n_txt = lax.axis_size("img"), lax.axis_size("txt")
    rows, cols = images.shape[0], texts.shape[0]
    part = images.shape[1]
    depth = part * n_txt
    batch = rows * n_img
    height = depth // SQUARE
    scale = jnp.exp(scale_logarithm)
    base = (lax.axis_index("txt") * cols).astype(jnp.int32).reshape(1)
    core = (lax.axis_index("img") % CORES).astype(jnp.int32).reshape(1)
    places = positive.reshape(1, rows)

    text_full = lax.all_gather(texts.T, "img", axis=0, tiled=True)

    def gather(block):
        by_pair = collect(block, "txt", Y_PAIRS, PAIRS)
        return stay(collect(by_pair, "txt", SQUARE, SQUARES))

    def none(block):
        return jnp.zeros((SQUARE, Y_PAIRS) + block.shape, block.dtype)

    always = scale[0] > -1.0
    image_full = lax.cond(always, gather, none, images.T)

    macs = rows * cols * depth
    logits, text_t, row_out, row_norm, row_mean, col_norm, col_mean, matched = call(
        lambda *refs: tile_kernel(*refs),
        "tile",
        [smem(), smem(), vmem(), vmem(), vmem()],
        [
            ((cols, rows), F32, vmem()),
            ((depth, cols), BF16, vmem()),
            ((n_txt, 1, rows), F32, vmem()),
            ((1, rows), F32, vmem()),
            ((1, rows), F32, vmem()),
            ((1, cols), F32, vmem()),
            ((1, cols), F32, vmem()),
            ((1, LANES), F32, vmem()),
        ],
        2 * macs, 6 << 20, 2 * rows * cols,
    )(scale, base, places, image_full, text_full)

    seen = exchange(row_out, "txt")
    row_norms, col_out = call(
        lambda *refs: rows_kernel(*refs),
        "rows",
        [vmem()] * 6,
        [((1, rows), F32, vmem()), ((n_img, 1, 2 * cols + LANES), F32, vmem())],
        8 * n_txt * rows, 1 << 18, n_txt * rows,
    )(seen, row_norm, row_mean, col_norm, col_mean, matched)

    seen = exchange(col_out, "img")
    weights, image_part = call(
        lambda *refs: weights_kernel(n_txt, *refs),
        "weights",
        [smem(), smem()] + [vmem()] * 5,
        [((cols, rows), BF16, vmem()), ((SQUARE, height + TAIL_ROWS, rows), BF16, hbm())],
        2 * macs, 6 << 20, 2 * rows * cols,
        [
            pltpu.VMEM((SQUARE, height + TAIL_ROWS, rows), BF16),
            pltpu.SemaphoreType.DMA((SQUARE // 2,)),
        ],
        48,
    )(scale, base, places, seen, row_norms, logits, text_t)

    half = (Z_CHIPS, depth // n_img, cols)
    own, other = call(
        lambda *refs: text_kernel(*refs),
        "texts",
        [smem(), smem(), vmem(), vmem()],
        [(half, BF16, vmem()), (half, BF16, vmem())],
        2 * macs, 4 << 20,
    )(scale, core, weights, image_full)
    swap = [(z * CORES + c, z * CORES + 1 - c) for z in range(Z_CHIPS) for c in range(CORES)]
    text_part = own.astype(F32) + lax.ppermute(other, "img", swap).astype(F32)
    grad_texts = lax.psum_scatter(
        text_part.astype(BF16).reshape(-1, cols),
        "img",
        scatter_dimension=0,
        axis_index_groups=ALONG_Z,
        tiled=True,
    ).T

    (partial,) = call(
        lambda *refs: square_kernel(*refs),
        "square",
        [vmem()],
        [((Y_PAIRS, part, rows + LANES), BF16, vmem())],
        depth * rows, 3 << 20,
    )(exchange(image_part, "txt", SQUARES))
    loss, grad_images, grad_log_scale = call(
        lambda *refs: pair_kernel(batch, *refs),
        "pair",
        [vmem()],
        [((1,), F32, smem()), ((part, rows), BF16, vmem()), ((1,), F32, smem())],
        Y_PAIRS * part * rows, 1 << 19,
    )(exchange(partial, "txt", PAIRS))
    return (loss, grad_images.T, grad_texts, grad_log_scale)


def solution(mesh):
    return jax.shard_map(
        per_device,
        mesh=mesh,
        in_specs=(P("img", "txt"), P("txt", "img"), P("img"), P()),
        out_specs=(P(), P("img", "txt"), P("txt", "img"), P()),
        check_vma=False,
    )
```

```python
import jax
import jax.numpy as jnp
from jax import lax
from jax.experimental import pallas as pl
from jax.experimental.pallas import tpu as pltpu
from jax.sharding import PartitionSpec as P

X_CHIPS = 4
Y_PAIRS = 4
Z_CHIPS = 8
CORES = 2
SQUARE = 2 * X_CHIPS
PAIRS = [
    [(x * Y_PAIRS + pair) * 2 + side for pair in range(Y_PAIRS)]
    for x in range(X_CHIPS)
    for side in range(2)
]
SQUARES = [
    [(x * Y_PAIRS + pair) * 2 + side for x in range(X_CHIPS) for side in range(2)]
    for pair in range(Y_PAIRS)
]
ALONG_Z = [[z * CORES + core for z in range(Z_CHIPS)] for core in range(CORES)]

LANES = 128
TAIL_ROWS = 8
F32 = jnp.float32
BF16 = jnp.bfloat16


def exchange(blocks, axis, groups=None):
    return lax.all_to_all(blocks, axis, 0, 0, axis_index_groups=groups)


def collect(block, axis, count, groups=None):
    return exchange(jnp.broadcast_to(block[None], (count,) + block.shape), axis, groups)


def vmem():
    return pl.BlockSpec(memory_space=pltpu.VMEM)


def hbm():
    return pl.BlockSpec(memory_space=pltpu.HBM)


def smem():
    return pl.BlockSpec(memory_space=pltpu.SMEM)


def call(kernel, name, in_specs, outs, flops, moved, powers=0, scratch=(), limit=48):
    out_shape = [jax.ShapeDtypeStruct(shape, dtype) for shape, dtype, _ in outs]
    run = pl.pallas_call(
        kernel,
        name=name,
        out_shape=out_shape,
        in_specs=in_specs,
        out_specs=[spec for _, _, spec in outs],
        scratch_shapes=list(scratch),
        compiler_params=pltpu.CompilerParams(vmem_limit_bytes=limit << 20),
        cost_estimate=pl.CostEstimate(flops=flops, bytes_accessed=moved, transcendentals=powers),
    )
    return lambda *operands: tuple(run(*operands))


def to_lanes(column):
    return jnp.broadcast_to(column, (LANES, LANES)).T[:1]


def to_sublanes(line):
    return jnp.broadcast_to(line, (LANES, LANES)).T[:, :1]


def pick(shape, axis, values):
    index = lax.broadcasted_iota(jnp.int32, shape, axis)
    out = jnp.zeros(shape, F32)
    for k, value in enumerate(values):
        out = jnp.where(index == k, value, out)
    return out


def thirds(value):
    first = value.astype(BF16).astype(F32)
    rest = value - first
    second = rest.astype(BF16).astype(F32)
    return [first, second, (rest - second).astype(BF16).astype(F32)]


def is_match(pos_ref, base_ref, start, rows):
    ids = lax.broadcasted_iota(jnp.int32, (LANES, rows), 0) + (base_ref[0] + start)
    return pos_ref[...] == ids


def stay(block):
    return pl.pallas_call(
        lambda block_ref, same_ref: None,
        name="stay",
        out_shape=jax.ShapeDtypeStruct(block.shape, block.dtype),
        in_specs=[hbm()],
        out_specs=hbm(),
        input_output_aliases={0: 0},
        compiler_params=pltpu.CompilerParams(vmem_limit_bytes=57 << 20),
    )(block)


def tile_kernel(
    scale_ref, base_ref, pos_ref, image_in, text_ref,
    logit_ref, text_out, row_out, row_norm, row_mean, col_norm, col_mean, matched_out,
    image_ref, image_sems,
):
    depth, cols = text_ref.shape
    rows = pos_ref.shape[1]
    half = SQUARE // 2
    reads = []
    for k in range(2):
        span = pl.ds(k * half, half)
        reads.append(
            pltpu.make_async_copy(image_in.at[span], image_ref.at[span], image_sems.at[k])
        )
        reads[-1].start()
    part = depth // (SQUARE * Y_PAIRS)
    for x in range(X_CHIPS):
        for side in range(2):
            for pair in range(Y_PAIRS):
                source = ((x * Y_PAIRS + pair) * 2 + side) * part
                target = ((x * 2 + side) * Y_PAIRS + pair) * part
                text_out[target : target + part, :] = text_ref[source : source + part, :]
    reads[0].wait()
    image_t = image_ref[:half].reshape(depth // 2, rows)
    for start in range(0, cols, LANES):
        span = slice(start, start + LANES)
        logit_ref[span, :] = lax.dot_general(
            text_out[: depth // 2, span], image_t, (((0,), (0,)), ((), ())),
            preferred_element_type=F32,
        )
    reads[1].wait()
    image_t = image_ref[half:].reshape(depth // 2, rows)
    row_high = jnp.full((1, rows), -jnp.inf, F32)
    matched = jnp.zeros((1, rows), F32)
    for start in range(0, cols, LANES):
        span = slice(start, start + LANES)
        logits = lax.dot_general(
            text_out[depth // 2 :, span], image_t, (((0,), (0,)), ((), ())),
            preferred_element_type=F32,
        )
        logits = scale_ref[0] * (logit_ref[span, :] + logits)
        logit_ref[span, :] = logits
        high = jnp.max(logits, axis=1, keepdims=True)
        powers = jnp.exp(logits - high)
        total = jnp.sum(powers, axis=1, keepdims=True)
        mean = jnp.sum(powers * logits, axis=1, keepdims=True) / total
        col_norm[:, span] = to_lanes(high + jnp.log(total))
        col_mean[:, span] = to_lanes(mean)
        row_high = jnp.maximum(row_high, jnp.max(logits, axis=0, keepdims=True))
        mask = is_match(pos_ref, base_ref, start, rows)
        matched += jnp.sum(jnp.where(mask, logits, 0.0), axis=0, keepdims=True)
    total = jnp.zeros((1, rows), F32)
    mean = jnp.zeros((1, rows), F32)
    for start in range(0, cols, LANES):
        logits = logit_ref[start : start + LANES, :]
        powers = jnp.exp(logits - row_high)
        total += jnp.sum(powers, axis=0, keepdims=True)
        mean += jnp.sum(powers * logits, axis=0, keepdims=True)
    norm = row_high + jnp.log(total)
    row_norm[...] = norm
    row_mean[...] = mean / total
    for k in range(row_out.shape[0]):
        row_out[k] = norm
    matched_out[...] = jnp.broadcast_to(jnp.sum(matched, axis=1, keepdims=True), (1, LANES))


def merge(norms):
    high = jnp.max(norms, axis=0, keepdims=True)
    return high + jnp.log(jnp.sum(jnp.exp(norms - high), axis=0, keepdims=True))


def rows_kernel(seen_ref, row_norm, row_mean, col_norm, col_mean, matched_ref, norm_out, col_out):
    norms = merge(seen_ref[:, 0, :])
    norm_out[...] = norms
    slope = jnp.sum(jnp.exp(row_norm[...] - norms) * row_mean[...], axis=1, keepdims=True)
    matched = matched_ref[:, :1]
    sums = [0.5 * jnp.sum(norms, axis=1, keepdims=True), 0.5 * slope - matched, matched]
    sums = pick((1, LANES), 1, sums)
    cols = col_norm.shape[1]
    for k in range(col_out.shape[0]):
        col_out[k, :, :cols] = col_norm[...]
        col_out[k, :, cols : 2 * cols] = col_mean[...]
        col_out[k, :, 2 * cols :] = sums


def weights_kernel(
    parts, scale_ref, base_ref, pos_ref, seen_ref, norm_ref, logit_ref, text_ref,
    weight_out, image_out, image_ref, image_sems,
):
    cols, rows = logit_ref.shape
    seen = seen_ref[:, 0, :cols]
    norms = merge(seen)
    slope = jnp.sum(jnp.exp(seen - norms) * seen_ref[:, 0, cols : 2 * cols], keepdims=True)
    sums = jnp.sum(seen_ref[:, 0, 2 * cols :], axis=0, keepdims=True)
    loss = 0.5 * jnp.sum(norms, axis=1, keepdims=True) - sums[:, 2:3] + sums[:, :1] / parts
    row_norms = norm_ref[...]
    for start in range(0, cols, LANES):
        span = slice(start, start + LANES)
        logits = logit_ref[span, :]
        col_norms = to_sublanes(norms[:, span])
        weights = 0.5 * (jnp.exp(logits - row_norms) + jnp.exp(logits - col_norms))
        mask = is_match(pos_ref, base_ref, start, rows)
        weight_out[span, :] = jnp.where(mask, weights - 1.0, weights).astype(BF16)
    height = text_ref.shape[0] // SQUARE
    pieces = thirds(loss) + thirds(0.5 * slope + sums[:, 1:2])
    tail = pick((TAIL_ROWS, rows), 0, pieces).astype(BF16)
    for k in range(SQUARE):
        image_ref[k, height:, :] = tail
    weights = weight_out[...]
    step = 2
    copies = []
    for first in range(0, SQUARE, step):
        grad = scale_ref[0] * jnp.dot(
            text_ref[first * height : (first + step) * height, :], weights,
            preferred_element_type=F32,
        )
        grad = grad.astype(BF16)
        for k in range(step):
            image_ref[first + k, :height, :] = grad[k * height : (k + 1) * height, :]
        span = pl.ds(first, step)
        copies.append(
            pltpu.make_async_copy(
                image_ref.at[span], image_out.at[span], image_sems.at[first // step]
            )
        )
        copies[-1].start()
    for copy in copies:
        copy.wait()


def text_kernel(scale_ref, core_ref, weight_ref, image_ref, own_out, other_out):
    rows = weight_ref.shape[1]
    weights = weight_ref[...]
    part = image_ref.shape[2]
    mine = core_ref[0] == 0
    step = 4
    for first in range(0, SQUARE, step):
        images = image_ref[first : first + step].reshape(step * Y_PAIRS * part, rows)
        grad = scale_ref[0] * lax.dot_general(
            images, weights, (((1,), (1,)), ((), ())), preferred_element_type=F32
        )
        grad = grad.astype(BF16)
        for k in range(step):
            x, side = divmod(first + k, 2)
            for pair in range(0, Y_PAIRS, CORES):
                z = (x * Y_PAIRS + pair) // CORES
                at = (k * Y_PAIRS + pair) * part
                even, odd = grad[at : at + part, :], grad[at + part : at + 2 * part, :]
                here = slice(side * part, (side + 1) * part)
                own_out[z, here, :] = jnp.where(mine, even, odd)
                other_out[z, here, :] = jnp.where(mine, odd, even)


def square_kernel(seen_ref, out_ref):
    height = seen_ref.shape[1] - TAIL_ROWS
    rows = seen_ref.shape[2]
    part = height // Y_PAIRS
    tail = jnp.sum(seen_ref[:, height:, :LANES].astype(F32), axis=0)
    loss = tail[0:1, :1] + tail[1:2, :1] + tail[2:3, :1]
    slope = tail[3:4, :1] + tail[4:5, :1] + tail[5:6, :1]
    tail = pick((part, LANES), 0, thirds(loss) + thirds(slope)).astype(BF16)
    for pair in range(Y_PAIRS):
        total = jnp.sum(seen_ref[:, pair * part : (pair + 1) * part, :].astype(F32), axis=0)
        out_ref[pair, :, :rows] = total.astype(BF16)
        out_ref[pair, :, rows:] = tail


def pair_kernel(batch, seen_ref, loss_ref, grad_ref, slope_ref):
    rows = grad_ref.shape[1]
    grad_ref[...] = jnp.sum(seen_ref[:, :, :rows].astype(F32), axis=0).astype(BF16)
    tail = jnp.sum(seen_ref[:, :, rows:].astype(F32), axis=0)
    loss_ref[0] = jnp.sum(tail[0:3, :1]) / batch
    slope_ref[0] = jnp.sum(tail[3:6, :1]) / batch


def per_device(images, texts, positive, scale_logarithm):
    n_img, n_txt = lax.axis_size("img"), lax.axis_size("txt")
    rows, cols = images.shape[0], texts.shape[0]
    part = images.shape[1]
    depth = part * n_txt
    batch = rows * n_img
    height = depth // SQUARE
    scale = jnp.exp(scale_logarithm)
    base = (lax.axis_index("txt") * cols).astype(jnp.int32).reshape(1)
    core = (lax.axis_index("img") % CORES).astype(jnp.int32).reshape(1)
    places = positive.reshape(1, rows)

    text_full = lax.all_gather(texts.T, "img", axis=0, tiled=True)

    def gather(block):
        by_pair = collect(block, "txt", Y_PAIRS, PAIRS)
        return stay(collect(by_pair, "txt", SQUARE, SQUARES))

    def none(block):
        return jnp.zeros((SQUARE, Y_PAIRS) + block.shape, block.dtype)

    always = scale[0] > -1.0
    image_full = lax.cond(always, gather, none, images.T)

    macs = rows * cols * depth
    logits, text_t, row_out, row_norm, row_mean, col_norm, col_mean, matched = call(
        lambda *refs: tile_kernel(*refs),
        "tile",
        [smem(), smem(), vmem(), hbm(), vmem()],
        [
            ((cols, rows), F32, vmem()),
            ((depth, cols), BF16, vmem()),
            ((n_txt, 1, rows), F32, vmem()),
            ((1, rows), F32, vmem()),
            ((1, rows), F32, vmem()),
            ((1, cols), F32, vmem()),
            ((1, cols), F32, vmem()),
            ((1, LANES), F32, vmem()),
        ],
        2 * macs, 6 << 20, 2 * rows * cols,
        [pltpu.VMEM(image_full.shape, BF16), pltpu.SemaphoreType.DMA((2,))],
    )(scale, base, places, image_full, text_full)

    seen = exchange(row_out, "txt")
    row_norms, col_out = call(
        lambda *refs: rows_kernel(*refs),
        "rows",
        [vmem()] * 6,
        [((1, rows), F32, vmem()), ((n_img, 1, 2 * cols + LANES), F32, vmem())],
        8 * n_txt * rows, 1 << 18, n_txt * rows,
    )(seen, row_norm, row_mean, col_norm, col_mean, matched)

    seen = exchange(col_out, "img")
    weights, image_part = call(
        lambda *refs: weights_kernel(n_txt, *refs),
        "weights",
        [smem(), smem()] + [vmem()] * 5,
        [((cols, rows), BF16, vmem()), ((SQUARE, height + TAIL_ROWS, rows), BF16, hbm())],
        2 * macs, 6 << 20, 2 * rows * cols,
        [
            pltpu.VMEM((SQUARE, height + TAIL_ROWS, rows), BF16),
            pltpu.SemaphoreType.DMA((SQUARE // 2,)),
        ],
        48,
    )(scale, base, places, seen, row_norms, logits, text_t)

    half = (Z_CHIPS, depth // n_img, cols)
    own, other = call(
        lambda *refs: text_kernel(*refs),
        "texts",
        [smem(), smem(), vmem(), vmem()],
        [(half, BF16, vmem()), (half, BF16, vmem())],
        2 * macs, 4 << 20,
    )(scale, core, weights, image_full)
    swap = [(z * CORES + c, z * CORES + 1 - c) for z in range(Z_CHIPS) for c in range(CORES)]
    text_part = own.astype(F32) + lax.ppermute(other, "img", swap).astype(F32)
    grad_texts = lax.psum_scatter(
        text_part.astype(BF16).reshape(-1, cols),
        "img",
        scatter_dimension=0,
        axis_index_groups=ALONG_Z,
        tiled=True,
    ).T

    (partial,) = call(
        lambda *refs: square_kernel(*refs),
        "square",
        [vmem()],
        [((Y_PAIRS, part, rows + LANES), BF16, vmem())],
        depth * rows, 3 << 20,
    )(exchange(image_part, "txt", SQUARES))
    loss, grad_images, grad_log_scale = call(
        lambda *refs: pair_kernel(batch, *refs),
        "pair",
        [vmem()],
        [((1,), F32, smem()), ((part, rows), BF16, vmem()), ((1,), F32, smem())],
        Y_PAIRS * part * rows, 1 << 19,
    )(exchange(partial, "txt", PAIRS))
    return (loss, grad_images.T, grad_texts, grad_log_scale)


def solution(mesh):
    return jax.shard_map(
        per_device,
        mesh=mesh,
        in_specs=(P("img", "txt"), P("txt", "img"), P("img"), P()),
        out_specs=(P(), P("img", "txt"), P("txt", "img"), P()),
        check_vma=False,
    )
```
